256 devices in a mesh: gx: 32 (over x, z_hi, y), gy: 8 (over z_lo, core).
Axes of the slice: x: 4, y: 4, z: 8 (z_hi: 2, z_lo: 4; z = z_hi * 4 + z_lo), core: 2. Of those that a mesh axis runs over, the one named last changes fastest.
Arguments:
- features: bfloat16 [131072, 256], P(('gx', 'gy')), may hold values from -6 to 6
- conv_weight: bfloat16 [27, 256, 256], replicated, may hold values from -0.078125 to 0.078125
- gamma: float32 [256], replicated, may hold values from 0.5 to 2
- beta: float32 [256], replicated, may hold values from -3 to 3
- cotangent: bfloat16 [131072, 256], P(('gx', 'gy')), may hold values from -6 to 6
- counts: int32 [256], P(('gx', 'gy')), may hold values from 256 to 512, as said below
- rim_rows: int32 [32768], P(('gx', 'gy')), may hold values from 0 to 511, as said below
- neighbours: int32 [27, 131072], P(None, ('gx', 'gy')), may hold values from 0 to 1664, as said below
Outputs:
- activated: bfloat16 [131072, 256], P(('gx', 'gy'))
- input_grad: bfloat16 [131072, 256], P(('gx', 'gy'))
- weight_grad: float32 [27, 256, 256], replicated
- gamma_grad: float32 [256], replicated
- beta_grad: float32 [256], replicated
The draws below stay inside these ranges and needn't reach their ends.
Inputs may be any that keep to these rules, and one draw needn't show every extreme that they name: `counts`: one device has exactly 512 occupied slots; every device has at least half of them. `rim_rows`: each entry is an occupied slot of its device. `neighbours`: an entry below 512 is an occupied slot of the same device; 1664 means no input voxel; other entries lie in the rim block (a, b) of the pool with a - 1, b - 1 the first two coordinates of the offset (k // 9 - 1, k // 3 % 3 - 1), which are not both zero, and that neighbour device exists. Unoccupied slots have no input voxels; offset 13 maps an occupied slot to itself.
All inputs are finite; a program needn't handle non-finite values.
Results may differ from the reference program's by a relative error of at most 0.019.
Values may be sent and summed in bfloat16 or wider, within the bound.
No kernel may reach another device: no remote copies, remote signals or barrier semaphores. Data moves between devices by JAX's collectives and lax.ppermute only.
A program may use at most 128 MiB of HBM per device.

```python
import jax
import jax.numpy as jnp
from jax import lax

CH = 256
KV = 27
V_DEV = 512
RIM = 128
VOX = 131072
N_GX = 32
N_GY = 8


def occupancy(key):
    devices = N_GX * N_GY
    base = jax.random.randint(jax.random.fold_in(key, 11), (devices,), V_DEV // 2, V_DEV + 1)
    full_dev = jax.random.randint(jax.random.fold_in(key, 12), (), 0, devices)
    return jnp.where(jnp.arange(devices) == full_dev, V_DEV, base).astype(jnp.int32)


def draw_counts(key, part):
    return occupancy(key)


def draw_rim_rows(key, part):
    filled = occupancy(key)
    key = jax.random.fold_in(key, 2)
    devices = N_GX * N_GY
    raw = jax.random.randint(key, (devices, RIM), 0, 1 << 30)
    rows = raw % filled[:, None]
    rows = rows.at[:, 0].set(filled - 1)
    rows = rows.at[:, 1].set(0)
    return rows.reshape(-1).astype(jnp.int32)


def draw_neighbours(key, part):
    filled = occupancy(key)
    key = jax.random.fold_in(key, 3)
    devices = N_GX * N_GY
    shape = (KV, devices, V_DEV)
    dev_ids = jnp.arange(devices)
    dev_x = dev_ids // N_GY
    dev_y = dev_ids % N_GY
    offsets = jnp.arange(KV)
    step_x = offsets // 9 - 1
    step_y = offsets // 3 % 3 - 1
    picker = jax.random.randint(jax.random.fold_in(key, 1), shape, 0, 20)
    local = jax.random.randint(jax.random.fold_in(key, 2), shape, 0, 1 << 30) % filled[None, :, None]
    slot = jax.random.randint(jax.random.fold_in(key, 3), shape, 0, RIM)
    near_x = dev_x[None, :, None] + step_x[:, None, None]
    near_y = dev_y[None, :, None] + step_y[:, None, None]
    exists = (near_x >= 0) & (near_x < N_GX) & (near_y >= 0) & (near_y < N_GY)
    sideways = ((step_x != 0) | (step_y != 0))[:, None, None]
    halo_value = V_DEV + ((step_x + 1) * 3 + (step_y + 1))[:, None, None] * RIM + slot
    missing = V_DEV + 9 * RIM
    value = jnp.where(picker < 14, local, missing)
    value = jnp.where(sideways & exists & (picker < 6), halo_value, value)
    rows = jnp.arange(V_DEV)[None, None, :]
    value = jnp.where((offsets == 13)[:, None, None], rows + jnp.zeros(shape, jnp.int32), value)
    occupied = rows < filled[None, :, None]
    value = jnp.where(occupied, value, missing)
    return value.reshape(KV, devices * V_DEV).astype(jnp.int32)


def block_scale(own_key, extent, shards, least, top_value):
    gain = 1.0
    for dim, parts in shards:
        heights = jax.random.uniform(jax.random.fold_in(jax.random.fold_in(own_key, 6), dim), (parts,), jnp.float32, least / len(shards), top_value / len(shards))
        gain = gain * jnp.repeat(jnp.exp(heights), extent[dim] // parts).reshape((-1,) + (1,) * (len(extent) - 1 - dim))
    return gain


def scatter_about(stream_key, extent, deviation, most, cuts=(), held_as=jnp.bfloat16):
    values = jax.random.normal(stream_key, extent, jnp.float32) * deviation
    if len(cuts) > 0:
        values = block_scale(stream_key, extent, cuts, -0.22, 0.18) * values
    return jnp.clip(values, min=-most, max=most).astype(held_as)


def setup_inputs(seed: int = 0) -> dict:
    streams_of = jax.random.split(jax.random.key(seed), 9)
    return {
        "features": scatter_about(streams_of[0], (VOX, CH), 1.0, 6.0, ((0, 256),)),
        "conv_weight": scatter_about(streams_of[1], (KV, CH, CH), (KV * CH) ** -0.5, 0.078125),
        "gamma": jnp.clip(jax.random.uniform(streams_of[2], (CH,), jnp.float32, 0.5, 2.0), 0.5, 2.0),
        "beta": scatter_about(streams_of[3], (CH,), 0.7, 3.0, (), jnp.float32),
        "cotangent": scatter_about(streams_of[4], (VOX, CH), 1.0, 6.0, ((0, 256),)),
        "counts": draw_counts(jax.random.fold_in(streams_of[8], 71), 0),
        "rim_rows": draw_rim_rows(jax.random.fold_in(streams_of[8], 71), 0),
        "neighbours": draw_neighbours(jax.random.fold_in(streams_of[8], 71), 0),
    }


def reference(features, conv_weight, gamma, beta, cotangent, counts, rim_rows, neighbours):
    devices = N_GX * N_GY
    width = features.shape[1]
    slots = V_DEV + 9 * RIM + 1
    feat = features.reshape(devices, V_DEV, width)
    rims = rim_rows.reshape(devices, RIM)
    rim_feat = jax.vmap(lambda table, rows: table[rows])(feat, rims)
    grid = rim_feat.reshape(N_GX, N_GY, RIM, width)
    padded = jnp.pad(grid, ((1, 1), (1, 1), (0, 0), (0, 0)))
    blocks = []
    for row_pos in range(3):
        for col_pos in range(3):
            blocks.append(padded[row_pos:row_pos + N_GX, col_pos:col_pos + N_GY])
    cycle = jnp.stack(blocks, axis=2).reshape(devices, 9 * RIM, width)
    pools = jnp.concatenate([feat, cycle, jnp.zeros((devices, 1, width), jnp.bfloat16)], axis=1)
    maps = neighbours.reshape(KV, devices, V_DEV).transpose(1, 0, 2)
    weight_f = conv_weight.astype(jnp.float32)

    def forward(item):
        pool, index = item
        gathered = pool[index].astype(jnp.float32)
        return jnp.einsum('kvc,kcd->vd', gathered, weight_f)
    pre_norm = lax.map(forward, (pools, maps))
    mask = (jnp.arange(V_DEV)[None, :] < counts[:, None]).astype(jnp.float32)[:, :, None]
    total = jnp.sum(counts).astype(jnp.float32)
    masked = mask * pre_norm
    average = lax.optimization_barrier(jnp.sum(masked, axis=(0, 1))) / total
    variance = lax.optimization_barrier(jnp.sum(masked * pre_norm, axis=(0, 1))) / total - average * average
    inv_std = 1.0 / jnp.sqrt(variance + 1e-05)
    centered = (pre_norm - average) * inv_std
    scaled = gamma * centered + beta
    activated = (mask * jax.nn.silu(scaled)).astype(jnp.bfloat16)
    sig = jax.nn.sigmoid(scaled)
    dscaled = mask * cotangent.reshape(devices, V_DEV, width).astype(jnp.float32) * sig * (1.0 + scaled * (1.0 - sig))
    beta_grad = lax.optimization_barrier(jnp.sum(dscaled, axis=(0, 1)))
    gamma_grad = lax.optimization_barrier(jnp.sum(dscaled * centered, axis=(0, 1)))
    dpre = (mask * gamma * inv_std * (dscaled - (beta_grad + centered * gamma_grad) / total)).astype(jnp.bfloat16)

    def backward(carry, item):
        pool, index, grad = item
        gathered = pool[index].astype(jnp.float32)
        grad_f = grad.astype(jnp.float32)
        carry = carry + jnp.einsum('kvc,vd->kcd', gathered, grad_f)
        contrib = jnp.einsum('vd,kcd->kvc', grad_f, weight_f)
        pool_grad = jax.ops.segment_sum(contrib.reshape(-1, width), index.reshape(-1), num_segments=slots)
        return (carry, pool_grad)
    weight_grad, pool_grads = lax.scan(backward, jnp.zeros((KV, width, width), jnp.float32), (pools, maps, dpre))
    returned = pool_grads[:, V_DEV:V_DEV + 9 * RIM].reshape(N_GX, N_GY, 3, 3, RIM, width)
    padded_back = jnp.pad(returned, ((1, 1), (1, 1), (0, 0), (0, 0), (0, 0), (0, 0)))
    back = jnp.zeros((N_GX, N_GY, RIM, width), jnp.float32)
    for row_pos in range(3):
        for col_pos in range(3):
            back = back + padded_back[2 - row_pos:2 - row_pos + N_GX, 2 - col_pos:2 - col_pos + N_GY, row_pos, col_pos]
    back = back.reshape(devices, RIM, width)
    rim_add = jax.vmap(lambda rows, vals: jnp.zeros((V_DEV, width), jnp.float32).at[rows].add(vals))(rims, back)
    input_grad = (pool_grads[:, :V_DEV] + rim_add).astype(jnp.bfloat16)
    return (activated.reshape(devices * V_DEV, width), input_grad.reshape(devices * V_DEV, width), weight_grad, gamma_grad, beta_grad)
```

```python
import functools

import jax
import jax.numpy as jnp
from jax import lax
from jax.experimental import pallas as pl
from jax.experimental.pallas import tpu as pltpu
from jax.sharding import Mesh, PartitionSpec as P

AXES = ("x", "zh", "y", "zl", "core")
SIZES = (4, 2, 4, 4, 2)
GX = ("x", "zh", "y")
GY = ("zl", "core")
PLANE = ("x", "y")
DEPTH = ("zh", "zl")
F32 = jnp.float32
BF16 = jnp.bfloat16


def params(mib):
    return pltpu.CompilerParams(vmem_limit_bytes=mib << 20)


def rows_of(first, second, dims):
    return lax.dot_general(first, second, (dims, ((), ())), preferred_element_type=F32)


def rim_kernel(rows_ref, feat_ref, rim_ref):
    slots = feat_ref.shape[0]
    rims = rim_ref.shape[0]
    slot = lax.broadcasted_iota(jnp.int32, (slots, rims), 0)
    hit = jnp.where(slot == rows_ref[...], 1.0, 0.0).astype(BF16)
    rim_ref[...] = rows_of(hit, feat_ref[...], ((0,), (0,))).astype(BF16)


def forward_kernel(near_ref, feat_ref, halo_ref, weight_ref, gathered_ref, pre_ref, stats_ref):
    step = pl.program_id(0)
    slots, width = feat_ref.shape
    rims = halo_ref.shape[1]
    pool = jnp.concatenate([feat_ref[...], halo_ref[0]], axis=0)
    lanes = lax.broadcasted_iota(jnp.int32, (slots, rims), 1)
    total = None
    for j in range(3):
        row = near_ref[0, j : j + 1, :]
        row = jnp.where(row >= slots, row - step * rims, row)
        column = jnp.transpose(jnp.broadcast_to(row, (rims, slots)))
        hits = [
            jnp.where(column == lanes + t * rims, 1.0, 0.0).astype(BF16)
            for t in range(slots // rims + 1)
        ]
        rows = jnp.dot(jnp.concatenate(hits, axis=1), pool, preferred_element_type=F32).astype(BF16)
        gathered_ref[0, :, j * width : (j + 1) * width] = rows
        part = jnp.dot(rows, weight_ref[j], preferred_element_type=F32)
        total = part if total is None else total + part

    @pl.when(step == 0)
    def _():
        pre_ref[...] = total

    @pl.when(step > 0)
    def _():
        pre_ref[...] += total

    @pl.when(step == pl.num_programs(0) - 1)
    def _():
        pre = pre_ref[...]
        stats_ref[0:1, :] = jnp.sum(pre, axis=0, keepdims=True)
        stats_ref[1:2, :] = jnp.sum(pre * pre, axis=0, keepdims=True)


def moments(sums_ref):
    sums = jnp.sum(sums_ref[...], axis=0)
    total = sums[2:3, :]
    average = sums[0:1, :] / total
    variance = sums[1:2, :] / total - average * average
    return average, 1.0 / jnp.sqrt(variance + 1e-05), total


def activation_kernel(
    count_ref, pre_ref, sums_ref, gamma_ref, beta_ref, cotangent_ref, active_ref, dscaled_ref, stats_ref
):
    slots = pre_ref.shape[0]
    average, inv_std, _ = moments(sums_ref)
    centered = (pre_ref[...] - average) * inv_std
    scaled = gamma_ref[...] * centered + beta_ref[...]
    sig = jax.nn.sigmoid(scaled)
    mask = lax.broadcasted_iota(jnp.int32, pre_ref.shape, 0) < count_ref[0]
    active_ref[...] = jnp.where(mask, scaled * sig, 0.0).astype(BF16)
    dscaled = jnp.where(mask, cotangent_ref[...].astype(F32) * sig * (1.0 + scaled * (1.0 - sig)), 0.0)
    dscaled_ref[...] = dscaled
    stats_ref[0:1, :] = jnp.sum(dscaled, axis=0, keepdims=True)
    stats_ref[1:2, :] = jnp.sum(dscaled * centered, axis=0, keepdims=True)


def weight_grad_kernel(
    count_ref, half_ref, pre_ref, dscaled_ref, sums_ref, gamma_ref, back_ref, gathered_ref, dpre_ref, keep_ref, send_ref, bn_ref, term
):
    step = pl.program_id(0)

    @pl.when(step == 0)
    def _():
        average, inv_std, total = moments(sums_ref)
        back = jnp.sum(back_ref[...], axis=0)
        bn_ref[...] = back
        centered = (pre_ref[...] - average) * inv_std
        grad = gamma_ref[...] * inv_std * (dscaled_ref[...] - (back[0:1, :] + centered * back[1:2, :]) / total)
        mask = lax.broadcasted_iota(jnp.int32, pre_ref.shape, 0) < count_ref[0]
        dpre_ref[...] = jnp.where(mask, grad, 0.0).astype(BF16)

    width = dpre_ref.shape[1]
    half = width // 2
    term[...] = rows_of(gathered_ref[0], dpre_ref[...], ((0,), (0,)))
    first = pl.multiple_of(half_ref[0] * half, half)
    other = pl.multiple_of((1 - half_ref[0]) * half, half)
    for j in range(3):
        keep_ref[j] = term[pl.ds(j * width + first, half), :].astype(BF16)
        send_ref[j] = term[pl.ds(j * width + other, half), :].astype(BF16)


def pool_grad_kernel(near_ref, dpre_ref, weight_ref, local_ref, halo_ref):
    step = pl.program_id(0)
    slots, width = dpre_ref.shape
    rims = halo_ref.shape[1]
    pool_rows = slots + rims
    slot = lax.broadcasted_iota(jnp.int32, (pool_rows, slots), 0)
    hits, contribs = [], []
    for j in range(3):
        row = near_ref[0, j : j + 1, :]
        row = jnp.where(row >= slots, row - step * rims, row)
        hits.append(jnp.where(slot == row, 1.0, 0.0).astype(BF16))
        contribs.append(rows_of(dpre_ref[...], weight_ref[j], ((1,), (1,))).astype(BF16))
    total = jnp.dot(
        jnp.concatenate(hits, axis=1), jnp.concatenate(contribs, axis=0), preferred_element_type=F32
    )
    halo_ref[0] = total[slots:, :].astype(BF16)

    @pl.when(step == 0)
    def _():
        local_ref[...] = total[:slots, :]

    @pl.when(step > 0)
    def _():
        local_ref[...] += total[:slots, :]


def input_grad_kernel(rows_ref, local_ref, final_ref, out_ref):
    slots = local_ref.shape[0]
    rims = final_ref.shape[0]
    slot = lax.broadcasted_iota(jnp.int32, (slots, rims), 0)
    hit = jnp.where(slot == rows_ref[...], 1.0, 0.0).astype(BF16)
    final = final_ref[...]
    high = final.astype(BF16)
    low = (final - high.astype(F32)).astype(BF16)
    added = jnp.dot(hit, high, preferred_element_type=F32) + jnp.dot(hit, low, preferred_element_type=F32)
    out_ref[...] = (local_ref[...] + added).astype(BF16)


def join_kernel(half_ref, own_ref, other_ref, out_ref):
    half = own_ref.shape[1]
    first = pl.multiple_of(half_ref[0] * half, half)
    second = pl.multiple_of((1 - half_ref[0]) * half, half)
    out_ref[:, pl.ds(first, half), :] = own_ref[...].astype(F32)
    out_ref[:, pl.ds(second, half), :] = other_ref[...].astype(F32)


def smem():
    return pl.BlockSpec(memory_space=pltpu.SMEM)


def whole(shape):
    return pl.BlockSpec(shape, lambda *_: (0,) * len(shape))


def passed(value, axes, count, steps):
    first, last = max(0, -steps), min(count, count - steps)
    return lax.ppermute(value, axes, [(i, i + steps) for i in range(first, last)])


def exchange(parts, axes):
    return lax.all_to_all(parts, axes, 0, 0)


def shown(part, axes, count):
    return exchange(jnp.broadcast_to(part[None], (count,) + part.shape), axes)


def sums_over_all(part):
    inner = jnp.sum(shown(part, ("zh", "zl", "core"), 16), axis=0)
    return shown(inner, PLANE, 16)


def on_device(features, conv_weight, gamma, beta, cotangent, counts, rim_rows, neighbours):
    slots, width = features.shape
    rims = rim_rows.shape[0]
    offsets = neighbours.shape[0]
    groups = offsets // 3
    half = width // 2
    core = lax.axis_index("core").astype(jnp.int32)[None]
    near = neighbours.reshape(groups, 3, slots)
    rows = rim_rows.reshape(1, rims)
    gamma_row = gamma.reshape(1, width)
    beta_row = beta.reshape(1, width)

    rim = pl.pallas_call(
        rim_kernel, out_shape=jax.ShapeDtypeStruct((rims, width), BF16), compiler_params=params(16)
    )(rows, features)
    column = jnp.stack([passed(rim, GX, 32, 1), rim, passed(rim, GX, 32, -1)])
    halo = jnp.stack([passed(column, GY, 8, 1), column, passed(column, GY, 8, -1)], axis=1)
    halo = halo.reshape(groups, rims, width)

    near_spec = pl.BlockSpec((1, 3, slots), lambda g: (g, 0, 0))
    halo_spec = pl.BlockSpec((1, rims, width), lambda g: (g, 0, 0))
    weight_spec = pl.BlockSpec((3, width, width), lambda g: (g, 0, 0))
    gathered_spec = pl.BlockSpec((1, slots, 3 * width), lambda g: (g, 0, 0))
    half_spec = pl.BlockSpec((3, half, width), lambda g: (g, 0, 0))
    gathered, pre, stats = pl.pallas_call(
        forward_kernel,
        grid=(groups,),
        in_specs=[near_spec, whole((slots, width)), halo_spec, weight_spec],
        out_specs=[gathered_spec, whole((slots, width)), whole((2, width))],
        out_shape=[
            jax.ShapeDtypeStruct((groups, slots, 3 * width), BF16),
            jax.ShapeDtypeStruct((slots, width), F32),
            jax.ShapeDtypeStruct((2, width), F32),
        ],
        compiler_params=params(32),
    )(near, features, halo, conv_weight)

    count_row = jnp.full((1, width), counts[0].astype(F32))
    sums = sums_over_all(jnp.concatenate([stats, count_row, jnp.zeros((1, width), F32)], axis=0))
    activated, dscaled, back = pl.pallas_call(
        activation_kernel,
        in_specs=[smem()] + [pl.BlockSpec(memory_space=pltpu.VMEM)] * 5,
        out_shape=[
            jax.ShapeDtypeStruct((slots, width), BF16),
            jax.ShapeDtypeStruct((slots, width), F32),
            jax.ShapeDtypeStruct((2, width), F32),
        ],
        compiler_params=params(16),
    )(counts, pre, sums, gamma_row, beta_row, cotangent)
    back_sums = sums_over_all(back)

    dpre, keep, send, bn_grads = pl.pallas_call(
        weight_grad_kernel,
        grid=(groups,),
        in_specs=[smem(), smem()]
        + [
            whole((slots, width)),
            whole((slots, width)),
            whole(sums.shape),
            whole((1, width)),
            whole(back_sums.shape),
            gathered_spec,
        ],
        out_specs=[whole((slots, width)), half_spec, half_spec, whole((2, width))],
        out_shape=[
            jax.ShapeDtypeStruct((slots, width), BF16),
            jax.ShapeDtypeStruct((offsets, half, width), BF16),
            jax.ShapeDtypeStruct((offsets, half, width), BF16),
            jax.ShapeDtypeStruct((2, width), F32),
        ],
        scratch_shapes=[pltpu.VMEM((3 * width, width), F32)],
        compiler_params=params(32),
    )(counts, core, pre, dscaled, sums, gamma_row, back_sums, gathered)

    local, partials = pl.pallas_call(
        pool_grad_kernel,
        grid=(groups,),
        in_specs=[near_spec, whole((slots, width)), weight_spec],
        out_specs=[whole((slots, width)), halo_spec],
        out_shape=[
            jax.ShapeDtypeStruct((slots, width), F32),
            jax.ShapeDtypeStruct((groups, rims, width), BF16),
        ],
        compiler_params=params(32),
    )(near, dpre, conv_weight)

    met = lax.ppermute(send, "core", [(0, 1), (1, 0)])
    mine = (keep.astype(F32) + met.astype(F32)).astype(BF16)
    plane_rows = offsets * half // 16
    depth_rows = -(-plane_rows // 64) * 8
    mine = exchange(mine.reshape(16, plane_rows, width), PLANE)
    mine = jnp.sum(mine.astype(F32), axis=0).astype(BF16)
    mine = jnp.pad(mine, ((0, 8 * depth_rows - plane_rows), (0, 0)))
    mine = exchange(mine.reshape(8, depth_rows, width), DEPTH)
    mine = jnp.sum(mine.astype(F32), axis=0).astype(BF16)
    mine = shown(mine, DEPTH, 8).reshape(8 * depth_rows, width)[:plane_rows]
    mine = shown(mine, PLANE, 16).reshape(offsets, half, width)
    other = lax.ppermute(mine, "core", [(0, 1), (1, 0)])
    weight_grad = pl.pallas_call(
        join_kernel,
        grid=(groups,),
        in_specs=[smem(), half_spec, half_spec],
        out_specs=weight_spec,
        out_shape=jax.ShapeDtypeStruct((offsets, width, width), F32),
        compiler_params=params(32),
    )(core, mine, other)

    partials = partials.reshape(3, 3, rims, width)
    strips = (
        partials[1].astype(F32)
        + passed(partials[2], GX, 32, 1).astype(F32)
        + passed(partials[0], GX, 32, -1).astype(F32)
    )
    final = (
        strips[1]
        + passed(strips[2].astype(BF16), GY, 8, 1).astype(F32)
        + passed(strips[0].astype(BF16), GY, 8, -1).astype(F32)
    )
    input_grad = pl.pallas_call(
        input_grad_kernel,
        out_shape=jax.ShapeDtypeStruct((slots, width), BF16),
        compiler_params=params(16),
    )(rows, local, final)
    return (activated, input_grad, weight_grad, bn_grads[1], bn_grads[0])


def solution(mesh):
    finer = Mesh(mesh.devices.reshape(SIZES), AXES)
    return jax.shard_map(
        on_device,
        mesh=finer,
        in_specs=(P(AXES, None), P(), P(), P(), P(AXES, None), P(AXES), P(AXES), P(None, AXES)),
        out_specs=(P(AXES, None), P(AXES, None), P(), P(), P()),
        check_vma=False,
    )
```

```python
import functools

import jax
import jax.numpy as jnp
from jax import lax
from jax.experimental import pallas as pl
from jax.experimental.pallas import tpu as pltpu
from jax.sharding import Mesh, PartitionSpec as P

AXES = ("x", "zh", "y", "zl", "core")
SIZES = (4, 2, 4, 4, 2)
GX = ("x", "zh", "y")
GY = ("zl", "core")
PLANE = ("x", "y")
DEPTH = ("zh", "zl")
F32 = jnp.float32
BF16 = jnp.bfloat16


def params(mib):
    return pltpu.CompilerParams(vmem_limit_bytes=mib << 20)


def rows_of(first, second, dims):
    return lax.dot_general(first, second, (dims, ((), ())), preferred_element_type=F32)


def rim_kernel(rows_hbm, feat_hbm, near_hbm, rim_ref, feat_t_ref, near_ref, rows_ref, feat_ref, sem):
    copies = [
        pltpu.make_async_copy(rows_hbm, rows_ref, sem.at[0]),
        pltpu.make_async_copy(feat_hbm, feat_ref, sem.at[1]),
        pltpu.make_async_copy(near_hbm, near_ref, sem.at[2]),
    ]
    for copy in copies:
        copy.start()
    slots = feat_ref.shape[0]
    rims = rim_ref.shape[0]
    copies[0].wait()
    slot = lax.broadcasted_iota(jnp.int32, (slots, rims), 0)
    hit = jnp.where(slot == rows_ref[...], 1.0, 0.0).astype(BF16)
    copies[1].wait()
    feat = feat_ref[...]
    rim_ref[...] = rows_of(hit, feat, ((0,), (0,))).astype(BF16)
    feat_t_ref[...] = jnp.transpose(feat)
    copies[2].wait()


def local_kernel(near_ref, feat_t, weight_hbm, part_ref, weight_t_ref, held, sem):
    groups = near_ref.shape[0] // 3
    width, slots = feat_t.shape
    half = width // 2
    offsets = 3 * groups
    copies = [
        pltpu.make_async_copy(
            weight_hbm.at[pl.ds(9 * i, 9)], held.at[pl.ds(9 * i, 9)], sem.at[i]
        )
        for i in range(groups // 3)
    ]
    for copy in copies:
        copy.start()
    slot = lax.broadcasted_iota(jnp.int32, (slots, slots), 0)

    def gather(g, carry):
        hits = [
            jnp.where(slot == near_ref[pl.ds(3 * g + j, 1), :], 1.0, 0.0).astype(BF16) for j in range(3)
        ]
        rows = jnp.dot(feat_t[...], jnp.concatenate(hits, axis=1), preferred_element_type=F32).astype(BF16)
        for j in range(3):
            at = pl.ds(pl.multiple_of((3 * g + j) * half, half), half)
            part_ref[0, at, :] = rows[:half, j * slots : (j + 1) * slots]
            part_ref[1, at, :] = rows[half:, j * slots : (j + 1) * slots]
        return carry

    lax.fori_loop(0, groups, gather, 0, unroll=True)
    for copy in copies:
        copy.wait()

    def turn(k, carry):
        for h in range(2):
            at = pl.ds(pl.multiple_of((h * offsets + k) * half, half), half)
            weight_t_ref[:, at] = jnp.transpose(held[k, h * half : (h + 1) * half, :])
        return carry

    lax.fori_loop(0, offsets, turn, 0, unroll=3)


def forward_kernel(near_ref, halo_ref, part_ref, weight_t_ref, gathered_hbm, pre_ref, stats_ref, whole_rows, sem):
    groups, rims, width = halo_ref.shape
    slots = near_ref.shape[1]
    half = width // 2
    offsets = 3 * groups
    slot = lax.broadcasted_iota(jnp.int32, (rims, slots), 0) + slots
    span = 3 * half

    def copy(g):
        at = pl.ds(pl.multiple_of(g * span, span), span)
        return pltpu.make_async_copy(whole_rows.at[:, at], gathered_hbm.at[:, at], sem.at[g])

    def gather(g, carry):
        halo_t = jnp.transpose(halo_ref[g])
        hits = [
            jnp.where(slot + g * rims == near_ref[pl.ds(3 * g + j, 1), :], 1.0, 0.0).astype(BF16)
            for j in range(3)
        ]
        rows = jnp.dot(halo_t, jnp.concatenate(hits, axis=1), preferred_element_type=F32).astype(BF16)
        for j in range(3):
            at = pl.ds(pl.multiple_of((3 * g + j) * half, half), half)
            for h in range(2):
                found = rows[h * half : (h + 1) * half, j * slots : (j + 1) * slots]
                whole_rows[h, at, :] = part_ref[h, at, :] + found
        copy(g).start()
        return carry

    lax.fori_loop(0, groups, gather, 0, unroll=True)
    pre_t = None
    for h in range(2):
        weight_t = weight_t_ref[:, h * offsets * half : (h + 1) * offsets * half]
        term = jnp.dot(weight_t, whole_rows[h], preferred_element_type=F32)
        pre_t = term if pre_t is None else pre_t + term
    pre = jnp.transpose(pre_t)
    pre_ref[...] = pre
    stats_ref[0:1, :] = jnp.sum(pre, axis=0, keepdims=True)
    stats_ref[1:2, :] = jnp.sum(pre * pre, axis=0, keepdims=True)
    lax.fori_loop(0, groups, lambda g, c: (copy(g).wait(), c)[1], 0)


def moments(sums_ref):
    sums = jnp.sum(sums_ref[...], axis=0)
    total = sums[2:3, :]
    average = sums[0:1, :] / total
    variance = sums[1:2, :] / total - average * average
    return average, 1.0 / jnp.sqrt(variance + 1e-05), total


def activation_kernel(
    count_ref, pre_ref, sums_ref, gamma_ref, beta_ref, cotangent_ref, active_ref, dscaled_ref, stats_ref
):
    slots = pre_ref.shape[0]
    average, inv_std, _ = moments(sums_ref)
    centered = (pre_ref[...] - average) * inv_std
    scaled = gamma_ref[...] * centered + beta_ref[...]
    sig = jax.nn.sigmoid(scaled)
    mask = lax.broadcasted_iota(jnp.int32, pre_ref.shape, 0) < count_ref[0]
    active_ref[...] = jnp.where(mask, scaled * sig, 0.0).astype(BF16)
    dscaled = jnp.where(mask, cotangent_ref[...].astype(F32) * sig * (1.0 + scaled * (1.0 - sig)), 0.0)
    dscaled_ref[...] = dscaled
    stats_ref[0:1, :] = jnp.sum(dscaled, axis=0, keepdims=True)
    stats_ref[1:2, :] = jnp.sum(dscaled * centered, axis=0, keepdims=True)


def half_copies(gathered_hbm, which, held, sem):
    span = held.shape[0] // 3
    return [
        pltpu.make_async_copy(
            gathered_hbm.at[which, pl.ds(i * span, span)], held.at[pl.ds(i * span, span)], sem.at[i]
        )
        for i in range(3)
    ]


def half_products(copies, held, dpre, out_ref):
    span = held.shape[0] // 3
    half = out_ref.shape[1]
    for i in range(3):
        copies[i].wait()
        term = jnp.dot(held[i * span : (i + 1) * span, :], dpre, preferred_element_type=F32)
        out_ref[i * (span // half) : (i + 1) * (span // half)] = term.astype(BF16).reshape(
            span // half, half, out_ref.shape[2]
        )


def weight_grad_kernel(
    half_ref, count_ref, pre_ref, dscaled_ref, sums_ref, gamma_ref, back_ref, gathered_hbm, dpre_ref, send_ref, bn_ref, held, sem
):
    copies = half_copies(gathered_hbm, 1 - half_ref[0], held, sem)
    for copy in copies:
        copy.start()
    average, inv_std, total = moments(sums_ref)
    back = jnp.sum(back_ref[...], axis=0)
    bn_ref[...] = back
    centered = (pre_ref[...] - average) * inv_std
    grad = gamma_ref[...] * inv_std * (dscaled_ref[...] - (back[0:1, :] + centered * back[1:2, :]) / total)
    mask = lax.broadcasted_iota(jnp.int32, pre_ref.shape, 0) < count_ref[0]
    dpre = jnp.where(mask, grad, 0.0).astype(BF16)
    dpre_ref[...] = dpre
    half_products(copies, held, dpre, send_ref)


def other_half_kernel(half_ref, gathered_hbm, dpre_ref, keep_ref, held, sem):
    copies = half_copies(gathered_hbm, half_ref[0], held, sem)
    for copy in copies:
        copy.start()
    half_products(copies, held, dpre_ref[...], keep_ref)


def pool_grad_kernel(near_ref, dpre_ref, weight_ref, local_ref, halo_ref):
    step = pl.program_id(0)
    slots, width = dpre_ref.shape
    rims = halo_ref.shape[1]
    pool_rows = slots + rims
    slot = lax.broadcasted_iota(jnp.int32, (pool_rows, slots), 0)
    hits, contribs = [], []
    for j in range(3):
        row = near_ref[pl.ds(3 * step + j, 1), :]
        row = jnp.where(row >= slots, row - step * rims, row)
        hits.append(jnp.where(slot == row, 1.0, 0.0).astype(BF16))
        contribs.append(rows_of(dpre_ref[...], weight_ref[j], ((1,), (1,))).astype(BF16))
    total = jnp.dot(
        jnp.concatenate(hits, axis=1), jnp.concatenate(contribs, axis=0), preferred_element_type=F32
    )
    halo_ref[0] = total[slots:, :].astype(BF16)

    @pl.when(step == 0)
    def _():
        local_ref[...] = total[:slots, :]

    @pl.when(step > 0)
    def _():
        local_ref[...] += total[:slots, :]


def input_grad_kernel(rows_ref, local_ref, final_ref, out_ref):
    slots = local_ref.shape[0]
    rims = final_ref.shape[0]
    slot = lax.broadcasted_iota(jnp.int32, (slots, rims), 0)
    hit = jnp.where(slot == rows_ref[...], 1.0, 0.0).astype(BF16)
    final = final_ref[...]
    high = final.astype(BF16)
    low = (final - high.astype(F32)).astype(BF16)
    added = jnp.dot(hit, high, preferred_element_type=F32) + jnp.dot(hit, low, preferred_element_type=F32)
    out_ref[...] = (local_ref[...] + added).astype(BF16)


def plane_sum_kernel(parts_hbm, out_ref, held, sem):
    count, rows, _ = held.shape
    span = count // 4
    copies = [
        pltpu.make_async_copy(
            parts_hbm.at[pl.ds(n * span, span)], held.at[pl.ds(n * span, span)], sem.at[n]
        )
        for n in range(4)
    ]
    for copy in copies:
        copy.start()
    out_ref[rows:, :] = jnp.zeros((out_ref.shape[0] - rows, out_ref.shape[1]), BF16)
    total = None
    for n in range(4):
        copies[n].wait()
        part = jnp.sum(held[n * span : (n + 1) * span].astype(F32), axis=0)
        total = part if total is None else total + part
    out_ref[:rows, :] = total.astype(BF16)


def put_rows(part_ref, place, out_hbm, wide, sem):
    half = part_ref.shape[1]
    count = part_ref.shape[0] // 3
    rows = pl.ds(pl.multiple_of(place * half, half), half)
    copies = []
    for n in range(3):
        at = pl.ds(n * count, count)
        wide[at] = part_ref[at].astype(F32)
        copies.append(pltpu.make_async_copy(wide.at[at], out_hbm.at[at, rows], sem.at[n]))
        copies[-1].start()
    for copy in copies:
        copy.wait()


def own_rows_kernel(half_ref, part_ref, out_hbm, wide, sem):
    put_rows(part_ref, half_ref[0], out_hbm, wide, sem)


def other_rows_kernel(half_ref, part_ref, held_hbm, out_hbm, wide, sem):
    put_rows(part_ref, 1 - half_ref[0], out_hbm, wide, sem)


def smem():
    return pl.BlockSpec(memory_space=pltpu.SMEM)


def whole(shape):
    return pl.BlockSpec(shape, lambda *_: (0,) * len(shape))


def passed(value, axes, count, steps):
    first, last = max(0, -steps), min(count, count - steps)
    return lax.ppermute(value, axes, [(i, i + steps) for i in range(first, last)])


def exchange(parts, axes):
    return lax.all_to_all(parts, axes, 0, 0)


def shown(part, axes, count):
    return exchange(jnp.broadcast_to(part[None], (count,) + part.shape), axes)


def sums_over_all(part):
    inner = jnp.sum(shown(part, ("zh", "zl", "core"), 16), axis=0)
    return shown(inner, PLANE, 16)


def vmem():
    return pl.BlockSpec(memory_space=pltpu.VMEM)


def hbm():
    return pl.BlockSpec(memory_space=pl.ANY)


def swapped(value):
    return lax.ppermute(value, "core", [(0, 1), (1, 0)])


def forward_local(near, feat_t, weight):
    offsets, slots = near.shape
    width = feat_t.shape[0]
    return pl.pallas_call(
        local_kernel,
        in_specs=[vmem(), vmem(), hbm()],
        out_specs=[vmem(), vmem()],
        out_shape=[
            jax.ShapeDtypeStruct((2, offsets * width // 2, slots), BF16),
            jax.ShapeDtypeStruct((width, offsets * width), BF16),
        ],
        scratch_shapes=[pltpu.VMEM((offsets, width, width), BF16), pltpu.SemaphoreType.DMA((3,))],
        compiler_params=params(24),
    )(near, feat_t, weight)


def forward_rest(near, halo, part, weight_t):
    slots = near.shape[1]
    groups, _, width = halo.shape
    return pl.pallas_call(
        forward_kernel,
        in_specs=[vmem()] * 4,
        out_specs=[hbm(), vmem(), vmem()],
        out_shape=[
            pltpu.HBM(part.shape, BF16),
            jax.ShapeDtypeStruct((slots, width), F32),
            jax.ShapeDtypeStruct((2, width), F32),
        ],
        scratch_shapes=[pltpu.VMEM(part.shape, BF16), pltpu.SemaphoreType.DMA((groups,))],
        compiler_params=params(24),
    )(near, halo, part, weight_t)


def weight_grad_sent(core, counts, pre, dscaled, sums, gamma_row, back_sums, gathered, offsets):
    slots, width = pre.shape
    return pl.pallas_call(
        weight_grad_kernel,
        in_specs=[smem(), smem()] + [vmem()] * 5 + [hbm()],
        out_specs=[vmem()] * 3,
        out_shape=[
            jax.ShapeDtypeStruct((slots, width), BF16),
            jax.ShapeDtypeStruct((offsets, width // 2, width), BF16),
            jax.ShapeDtypeStruct((2, width), F32),
        ],
        scratch_shapes=[pltpu.VMEM(gathered.shape[1:], BF16), pltpu.SemaphoreType.DMA((3,))],
        compiler_params=params(16),
    )(core, counts, pre, dscaled, sums, gamma_row, back_sums, gathered)


def weight_grad_kept(core, gathered, dpre, offsets):
    width = dpre.shape[1]
    return pl.pallas_call(
        other_half_kernel,
        in_specs=[smem(), hbm(), vmem()],
        out_specs=vmem(),
        out_shape=jax.ShapeDtypeStruct((offsets, width // 2, width), BF16),
        scratch_shapes=[pltpu.VMEM(gathered.shape[1:], BF16), pltpu.SemaphoreType.DMA((3,))],
        compiler_params=params(16),
    )(core, gathered, dpre)


def widened(core, part, held):
    offsets, half, width = part.shape
    rest = [] if held is None else [held]
    return pl.pallas_call(
        own_rows_kernel if held is None else other_rows_kernel,
        in_specs=[smem(), vmem()] + [hbm()] * len(rest),
        out_specs=hbm(),
        out_shape=pltpu.HBM((offsets, 2 * half, width), F32),
        scratch_shapes=[pltpu.VMEM(part.shape, F32), pltpu.SemaphoreType.DMA((3,))],
        input_output_aliases={2: 0} if rest else {},
        compiler_params=params(16),
    )(core, part, *rest)


def pool_gradient(near, dpre, weight):
    offsets, slots = near.shape
    groups = offsets // 3
    width = dpre.shape[1]
    rims = slots // 4
    return pl.pallas_call(
        pool_grad_kernel,
        grid=(groups,),
        in_specs=[
            whole(near.shape),
            whole((slots, width)),
            pl.BlockSpec((3, width, width), lambda g: (g, 0, 0)),
        ],
        out_specs=[whole((slots, width)), pl.BlockSpec((1, rims, width), lambda g: (g, 0, 0))],
        out_shape=[
            jax.ShapeDtypeStruct((slots, width), F32),
            jax.ShapeDtypeStruct((groups, rims, width), BF16),
        ],
        compiler_params=params(20),
    )(near, dpre, weight)


def on_device(features, conv_weight, gamma, beta, cotangent, counts, rim_rows, neighbours):
    slots, width = features.shape
    rims = rim_rows.shape[0]
    offsets = neighbours.shape[0]
    groups = offsets // 3
    half = width // 2
    core = lax.axis_index("core").astype(jnp.int32)[None]
    rows = rim_rows.reshape(1, rims)
    gamma_row = gamma.reshape(1, width)
    beta_row = beta.reshape(1, width)
    weight = pltpu.with_memory_space_constraint(conv_weight, pltpu.HBM)

    rim, feat_t, near = pl.pallas_call(
        rim_kernel,
        in_specs=[hbm()] * 3,
        out_specs=[vmem()] * 3,
        out_shape=[
            jax.ShapeDtypeStruct((rims, width), BF16),
            jax.ShapeDtypeStruct((width, slots), BF16),
            jax.ShapeDtypeStruct((offsets, slots), jnp.int32),
        ],
        scratch_shapes=[
            pltpu.VMEM((1, rims), jnp.int32),
            pltpu.VMEM((slots, width), BF16),
            pltpu.SemaphoreType.DMA((3,)),
        ],
        compiler_params=params(16),
    )(
        pltpu.with_memory_space_constraint(rows, pltpu.HBM),
        pltpu.with_memory_space_constraint(features, pltpu.HBM),
        pltpu.with_memory_space_constraint(neighbours, pltpu.HBM),
    )
    below, above = passed(rim, GX, 32, 1), passed(rim, GX, 32, -1)
    part, weight_t = forward_local(near, feat_t, weight)
    below, above, part, weight_t = lax.optimization_barrier((below, above, part, weight_t))
    column = jnp.stack([below, rim, above])
    halo = jnp.stack([passed(column, GY, 8, 1), column, passed(column, GY, 8, -1)], axis=1)
    halo = halo.reshape(groups, rims, width)
    gathered, pre, stats = forward_rest(near, halo, part, weight_t)

    count_row = jnp.full((1, width), counts[0].astype(F32))
    sums = sums_over_all(jnp.concatenate([stats, count_row, jnp.zeros((1, width), F32)], axis=0))
    activated, dscaled, back = pl.pallas_call(
        activation_kernel,
        in_specs=[smem()] + [vmem()] * 5,
        out_shape=[
            jax.ShapeDtypeStruct((slots, width), BF16),
            jax.ShapeDtypeStruct((slots, width), F32),
            jax.ShapeDtypeStruct((2, width), F32),
        ],
        compiler_params=params(16),
    )(counts, pre, sums, gamma_row, beta_row, cotangent)
    back_sums = sums_over_all(back)

    gathered = pltpu.with_memory_space_constraint(gathered, pltpu.HBM)
    dpre, send, bn_grads = weight_grad_sent(
        core, counts, pre, dscaled, sums, gamma_row, back_sums, gathered, offsets
    )
    met = swapped(send)
    keep = weight_grad_kept(core, gathered, dpre, offsets)
    keep, met = lax.optimization_barrier((keep, met))
    mine = (keep.astype(F32) + met.astype(F32)).astype(BF16).reshape(offsets * half, width)

    plane_rows = offsets * half // 16
    depth_rows = -(-plane_rows // 64) * 8
    mine = exchange(mine.reshape(16, plane_rows, width), PLANE)
    local, partials = pool_gradient(near, dpre, weight)
    gamma_grad, beta_grad = bn_grads[1], bn_grads[0]
    mine, local, gamma_grad, beta_grad = lax.optimization_barrier((mine, local, gamma_grad, beta_grad))
    mine = pl.pallas_call(
        plane_sum_kernel,
        in_specs=[hbm()],
        out_specs=vmem(),
        out_shape=jax.ShapeDtypeStruct((8 * depth_rows, width), BF16),
        scratch_shapes=[pltpu.VMEM((16, plane_rows, width), BF16), pltpu.SemaphoreType.DMA((4,))],
        compiler_params=params(16),
    )(pltpu.with_memory_space_constraint(mine, pltpu.HBM))
    mine = exchange(mine.reshape(8, depth_rows, width), DEPTH)
    mine = jnp.sum(mine.astype(F32), axis=0).astype(BF16)
    mine = shown(mine, DEPTH, 8).reshape(8 * depth_rows, width)[:plane_rows]
    mine, partials = lax.optimization_barrier((mine, partials))
    partials = partials.reshape(3, 3, rims, width)
    below, above = passed(partials[2], GX, 32, 1), passed(partials[0], GX, 32, -1)
    strips = partials[1].astype(F32) + below.astype(F32) + above.astype(F32)
    left = passed(strips[2].astype(BF16), GY, 8, 1)
    right = passed(strips[0].astype(BF16), GY, 8, -1)
    mine = shown(mine, PLANE, 16).reshape(offsets, half, width)
    final = strips[1] + left.astype(F32) + right.astype(F32)
    input_grad = pl.pallas_call(
        input_grad_kernel,
        out_shape=jax.ShapeDtypeStruct((slots, width), BF16),
        compiler_params=params(16),
    )(rows, local, final)
    mine, input_grad = lax.optimization_barrier((mine, input_grad))
    other = swapped(mine)
    held = widened(core, mine, None)
    other, held = lax.optimization_barrier((other, held))
    weight_grad = widened(core, other, held)
    return (activated, input_grad, weight_grad, gamma_grad, beta_grad)


def solution(mesh):
    finer = Mesh(mesh.devices.reshape(SIZES), AXES)
    return jax.shard_map(
        on_device,
        mesh=finer,
        in_specs=(P(AXES, None), P(), P(), P(), P(AXES, None), P(AXES), P(AXES), P(None, AXES)),
        out_specs=(P(AXES, None), P(AXES, None), P(), P(), P()),
        check_vma=False,
    )
```

```python
import functools

import jax
import jax.numpy as jnp
from jax import lax
from jax.experimental import pallas as pl
from jax.experimental.pallas import tpu as pltpu
from jax.sharding import Mesh, PartitionSpec as P

AXES = ("x", "zh", "y", "zl", "core")
SIZES = (4, 2, 4, 4, 2)
GX = ("x", "zh", "y")
GY = ("zl", "core")
PLANE = ("x", "y")
DEPTH = ("zh", "zl")
F32 = jnp.float32
BF16 = jnp.bfloat16


def params(mib):
    return pltpu.CompilerParams(vmem_limit_bytes=mib << 20)


def rows_of(first, second, dims):
    return lax.dot_general(first, second, (dims, ((), ())), preferred_element_type=F32)


def rim_kernel(rows_hbm, feat_hbm, near_hbm, rim_ref, feat_t_ref, near_ref, rows_ref, feat_ref, sem):
    copies = [
        pltpu.make_async_copy(rows_hbm, rows_ref, sem.at[0]),
        pltpu.make_async_copy(feat_hbm, feat_ref, sem.at[1]),
        pltpu.make_async_copy(near_hbm, near_ref, sem.at[2]),
    ]
    for copy in copies:
        copy.start()
    slots = feat_ref.shape[0]
    rims = rim_ref.shape[0]
    copies[0].wait()
    slot = lax.broadcasted_iota(jnp.int32, (slots, rims), 0)
    hit = jnp.where(slot == rows_ref[...], 1.0, 0.0).astype(BF16)
    copies[1].wait()
    feat = feat_ref[...]
    rim_ref[...] = rows_of(hit, feat, ((0,), (0,))).astype(BF16)
    feat_t_ref[...] = jnp.transpose(feat)
    copies[2].wait()


def local_kernel(near_ref, feat_t, weight_hbm, part_ref, weight_t_ref, held, sem):
    groups = near_ref.shape[0] // 3
    width, slots = feat_t.shape
    half = width // 2
    offsets = 3 * groups
    copies = [
        pltpu.make_async_copy(
            weight_hbm.at[pl.ds(9 * i, 9)], held.at[pl.ds(9 * i, 9)], sem.at[i]
        )
        for i in range(groups // 3)
    ]
    for copy in copies:
        copy.start()
    slot = lax.broadcasted_iota(jnp.int32, (slots, slots), 0)

    def gather(g, carry):
        hits = [
            jnp.where(slot == near_ref[pl.ds(3 * g + j, 1), :], 1.0, 0.0).astype(BF16) for j in range(3)
        ]
        rows = jnp.dot(feat_t[...], jnp.concatenate(hits, axis=1), preferred_element_type=F32).astype(BF16)
        for j in range(3):
            at = pl.ds(pl.multiple_of((3 * g + j) * half, half), half)
            part_ref[0, at, :] = rows[:half, j * slots : (j + 1) * slots]
            part_ref[1, at, :] = rows[half:, j * slots : (j + 1) * slots]
        return carry

    lax.fori_loop(0, groups, gather, 0, unroll=True)
    for copy in copies:
        copy.wait()

    def turn(k, carry):
        for h in range(2):
            at = pl.ds(pl.multiple_of((h * offsets + k) * half, half), half)
            weight_t_ref[:, at] = jnp.transpose(held[k, h * half : (h + 1) * half, :])
        return carry

    lax.fori_loop(0, offsets, turn, 0, unroll=3)


def column_kernel(odd_ref, rim_ref, first_ref, second_ref, column_ref):
    column_ref[1] = rim_ref[...]

    @pl.when(odd_ref[0] == 1)
    def _():
        column_ref[0] = first_ref[...]
        column_ref[2] = second_ref[...]

    @pl.when(odd_ref[0] == 0)
    def _():
        column_ref[0] = second_ref[...]
        column_ref[2] = first_ref[...]


def forward_kernel(
    odd_ref, near_ref, column_ref, first_ref, second_ref, part_ref, weight_t_ref, gathered_hbm, pre_ref, stats_ref, halo_ref, whole_rows, sem
):
    groups, rims, width = halo_ref.shape
    for a in range(3):
        halo_ref[3 * a + 1] = column_ref[a]

    @pl.when(odd_ref[0] == 1)
    def _():
        for a in range(3):
            halo_ref[3 * a] = first_ref[a]
            halo_ref[3 * a + 2] = second_ref[a]

    @pl.when(odd_ref[0] == 0)
    def _():
        for a in range(3):
            halo_ref[3 * a] = second_ref[a]
            halo_ref[3 * a + 2] = first_ref[a]

    slots = near_ref.shape[1]
    half = width // 2
    offsets = 3 * groups
    slot = lax.broadcasted_iota(jnp.int32, (rims, slots), 0) + slots
    span = 3 * half

    def copy(g):
        at = pl.ds(pl.multiple_of(g * span, span), span)
        return pltpu.make_async_copy(whole_rows.at[:, at], gathered_hbm.at[:, at], sem.at[g])

    def gather(g, carry):
        halo_t = jnp.transpose(halo_ref[g])
        hits = [
            jnp.where(slot + g * rims == near_ref[pl.ds(3 * g + j, 1), :], 1.0, 0.0).astype(BF16)
            for j in range(3)
        ]
        rows = jnp.dot(halo_t, jnp.concatenate(hits, axis=1), preferred_element_type=F32).astype(BF16)
        for j in range(3):
            at = pl.ds(pl.multiple_of((3 * g + j) * half, half), half)
            for h in range(2):
                found = rows[h * half : (h + 1) * half, j * slots : (j + 1) * slots]
                whole_rows[h, at, :] = part_ref[h, at, :] + found
        copy(g).start()
        return carry

    lax.fori_loop(0, groups, gather, 0, unroll=True)
    pre_t = None
    for h in range(2):
        weight_t = weight_t_ref[:, h * offsets * half : (h + 1) * offsets * half]
        term = jnp.dot(weight_t, whole_rows[h], preferred_element_type=F32)
        pre_t = term if pre_t is None else pre_t + term
    pre = jnp.transpose(pre_t)
    pre_ref[...] = pre
    stats_ref[0:1, :] = jnp.sum(pre, axis=0, keepdims=True)
    stats_ref[1:2, :] = jnp.sum(pre * pre, axis=0, keepdims=True)
    lax.fori_loop(0, groups, lambda g, c: (copy(g).wait(), c)[1], 0)


def moments(sums_ref):
    sums = jnp.sum(sums_ref[...], axis=0)
    total = sums[2:3, :]
    average = sums[0:1, :] / total
    variance = sums[1:2, :] / total - average * average
    return average, 1.0 / jnp.sqrt(variance + 1e-05), total


def activation_kernel(
    count_ref, pre_ref, sums_ref, gamma_ref, beta_ref, cotangent_ref, active_ref, dscaled_ref, stats_ref
):
    slots = pre_ref.shape[0]
    average, inv_std, _ = moments(sums_ref)
    centered = (pre_ref[...] - average) * inv_std
    scaled = gamma_ref[...] * centered + beta_ref[...]
    sig = jax.nn.sigmoid(scaled)
    mask = lax.broadcasted_iota(jnp.int32, pre_ref.shape, 0) < count_ref[0]
    active_ref[...] = jnp.where(mask, scaled * sig, 0.0).astype(BF16)
    dscaled = jnp.where(mask, cotangent_ref[...].astype(F32) * sig * (1.0 + scaled * (1.0 - sig)), 0.0)
    dscaled_ref[...] = dscaled
    stats_ref[0:1, :] = jnp.sum(dscaled, axis=0, keepdims=True)
    stats_ref[1:2, :] = jnp.sum(dscaled * centered, axis=0, keepdims=True)


def half_copies(gathered_hbm, which, held, sem):
    span = held.shape[0] // 3
    return [
        pltpu.make_async_copy(
            gathered_hbm.at[which, pl.ds(i * span, span)], held.at[pl.ds(i * span, span)], sem.at[i]
        )
        for i in range(3)
    ]


def half_products(copies, held, dpre, out_ref):
    span = held.shape[0] // 3
    half = out_ref.shape[1]
    for i in range(3):
        copies[i].wait()
        term = jnp.dot(held[i * span : (i + 1) * span, :], dpre, preferred_element_type=F32)
        out_ref[i * (span // half) : (i + 1) * (span // half)] = term.astype(BF16).reshape(
            span // half, half, out_ref.shape[2]
        )


def weight_grad_kernel(
    half_ref, count_ref, pre_ref, dscaled_ref, sums_ref, gamma_ref, back_ref, gathered_hbm, dpre_ref, send_ref, bn_ref, held, sem
):
    copies = half_copies(gathered_hbm, 1 - half_ref[0], held, sem)
    for copy in copies:
        copy.start()
    average, inv_std, total = moments(sums_ref)
    back = jnp.sum(back_ref[...], axis=0)
    bn_ref[...] = back
    centered = (pre_ref[...] - average) * inv_std
    grad = gamma_ref[...] * inv_std * (dscaled_ref[...] - (back[0:1, :] + centered * back[1:2, :]) / total)
    mask = lax.broadcasted_iota(jnp.int32, pre_ref.shape, 0) < count_ref[0]
    dpre = jnp.where(mask, grad, 0.0).astype(BF16)
    dpre_ref[...] = dpre
    half_products(copies, held, dpre, send_ref)


def other_half_kernel(half_ref, gathered_hbm, dpre_ref, keep_ref, held, sem):
    copies = half_copies(gathered_hbm, half_ref[0], held, sem)
    for copy in copies:
        copy.start()
    half_products(copies, held, dpre_ref[...], keep_ref)


def pool_grad_kernel(odd_ref, near_ref, dpre_ref, weight_ref, local_ref, halo_ref):
    step = pl.program_id(0)
    slots, width = dpre_ref.shape
    rims = halo_ref.shape[1]
    pool_rows = slots + rims
    slot = lax.broadcasted_iota(jnp.int32, (pool_rows, slots), 0)
    hits, contribs = [], []
    for j in range(3):
        row = near_ref[pl.ds(3 * step + j, 1), :]
        row = jnp.where(row >= slots, row - step * rims, row)
        hits.append(jnp.where(slot == row, 1.0, 0.0).astype(BF16))
        contribs.append(rows_of(dpre_ref[...], weight_ref[j], ((1,), (1,))).astype(BF16))
    total = jnp.dot(
        jnp.concatenate(hits, axis=1), jnp.concatenate(contribs, axis=0), preferred_element_type=F32
    )
    halo_ref[0] = total[slots:, :].astype(BF16)

    @pl.when(step == 0)
    def _():
        local_ref[...] = total[:slots, :]

    @pl.when(step > 0)
    def _():
        local_ref[...] += total[:slots, :]


def strip_kernel(odd_ref, parts_ref, first_ref, second_ref, strip_ref, out_first_ref, out_second_ref):
    strips = [
        parts_ref[3 + a].astype(F32) + first_ref[a].astype(F32) + second_ref[a].astype(F32)
        for a in range(3)
    ]
    strip_ref[...] = strips[1]
    odd = odd_ref[0] == 1
    out_first_ref[...] = jnp.where(odd, strips[0], strips[2]).astype(BF16)
    out_second_ref[...] = jnp.where(odd, strips[2], strips[0]).astype(BF16)


def input_grad_kernel(rows_ref, local_ref, strip_ref, first_ref, second_ref, out_ref):
    slots = local_ref.shape[0]
    rims = strip_ref.shape[0]
    slot = lax.broadcasted_iota(jnp.int32, (slots, rims), 0)
    hit = jnp.where(slot == rows_ref[...], 1.0, 0.0).astype(BF16)
    final = strip_ref[...] + first_ref[...].astype(F32) + second_ref[...].astype(F32)
    high = final.astype(BF16)
    low = (final - high.astype(F32)).astype(BF16)
    added = jnp.dot(hit, high, preferred_element_type=F32) + jnp.dot(hit, low, preferred_element_type=F32)
    out_ref[...] = (local_ref[...] + added).astype(BF16)


def plane_sum_kernel(parts_hbm, out_ref, held, sem):
    count, rows, _ = held.shape
    span = count // 4
    copies = [
        pltpu.make_async_copy(
            parts_hbm.at[pl.ds(n * span, span)], held.at[pl.ds(n * span, span)], sem.at[n]
        )
        for n in range(4)
    ]
    for copy in copies:
        copy.start()
    out_ref[rows:, :] = jnp.zeros((out_ref.shape[0] - rows, out_ref.shape[1]), BF16)
    total = None
    for n in range(4):
        copies[n].wait()
        part = jnp.sum(held[n * span : (n + 1) * span].astype(F32), axis=0)
        total = part if total is None else total + part
    out_ref[:rows, :] = total.astype(BF16)


def put_rows(part_ref, place, out_hbm, wide, sem):
    half = part_ref.shape[1]
    count = part_ref.shape[0] // 3
    rows = pl.ds(pl.multiple_of(place * half, half), half)
    copies = []
    for n in range(3):
        at = pl.ds(n * count, count)
        wide[at] = part_ref[at].astype(F32)
        copies.append(pltpu.make_async_copy(wide.at[at], out_hbm.at[at, rows], sem.at[n]))
        copies[-1].start()
    for copy in copies:
        copy.wait()


def own_rows_kernel(half_ref, part_ref, out_hbm, wide, sem):
    put_rows(part_ref, half_ref[0], out_hbm, wide, sem)


def other_rows_kernel(half_ref, part_ref, held_hbm, out_hbm, wide, sem):
    put_rows(part_ref, 1 - half_ref[0], out_hbm, wide, sem)


def smem():
    return pl.BlockSpec(memory_space=pltpu.SMEM)


def whole(shape):
    return pl.BlockSpec(shape, lambda *_: (0,) * len(shape))


def swaps(first, second, axes, count):
    met = []
    for value, start in ((first, 0), (second, 1)):
        edges = [(i, i + 1) for i in range(start, count - 1, 2)]
        met.append(lax.ppermute(value, axes, edges + [(j, i) for i, j in edges]))
    return met


def exchange(parts, axes):
    return lax.all_to_all(parts, axes, 0, 0)


def shown(part, axes, count):
    return exchange(jnp.broadcast_to(part[None], (count,) + part.shape), axes)


def sums_over_all(part):
    inner = jnp.sum(shown(part, ("zh", "zl", "core"), 16), axis=0)
    return shown(inner, PLANE, 16)


def vmem():
    return pl.BlockSpec(memory_space=pltpu.VMEM)


def hbm():
    return pl.BlockSpec(memory_space=pl.ANY)


def swapped(value):
    return lax.ppermute(value, "core", [(0, 1), (1, 0)])


def forward_local(near, feat_t, weight):
    offsets, slots = near.shape
    width = feat_t.shape[0]
    return pl.pallas_call(
        local_kernel,
        in_specs=[vmem(), vmem(), hbm()],
        out_specs=[vmem(), vmem()],
        out_shape=[
            jax.ShapeDtypeStruct((2, offsets * width // 2, slots), BF16),
            jax.ShapeDtypeStruct((width, offsets * width), BF16),
        ],
        scratch_shapes=[pltpu.VMEM((offsets, width, width), BF16), pltpu.SemaphoreType.DMA((3,))],
        compiler_params=params(24),
    )(near, feat_t, weight)


def forward_rest(odd, near, column, first, second, part, weight_t):
    offsets, slots = near.shape
    _, rims, width = column.shape
    groups = offsets // 3
    return pl.pallas_call(
        forward_kernel,
        in_specs=[smem()] + [vmem()] * 6,
        out_specs=[hbm(), vmem(), vmem()],
        out_shape=[
            pltpu.HBM(part.shape, BF16),
            jax.ShapeDtypeStruct((slots, width), F32),
            jax.ShapeDtypeStruct((2, width), F32),
        ],
        scratch_shapes=[
            pltpu.VMEM((groups, rims, width), BF16),
            pltpu.VMEM(part.shape, BF16),
            pltpu.SemaphoreType.DMA((groups,)),
        ],
        compiler_params=params(24),
    )(odd, near, column, first, second, part, weight_t)


def weight_grad_sent(core, counts, pre, dscaled, sums, gamma_row, back_sums, gathered, offsets):
    slots, width = pre.shape
    return pl.pallas_call(
        weight_grad_kernel,
        in_specs=[smem(), smem()] + [vmem()] * 5 + [hbm()],
        out_specs=[vmem()] * 3,
        out_shape=[
            jax.ShapeDtypeStruct((slots, width), BF16),
            jax.ShapeDtypeStruct((offsets, width // 2, width), BF16),
            jax.ShapeDtypeStruct((2, width), F32),
        ],
        scratch_shapes=[pltpu.VMEM(gathered.shape[1:], BF16), pltpu.SemaphoreType.DMA((3,))],
        compiler_params=params(16),
    )(core, counts, pre, dscaled, sums, gamma_row, back_sums, gathered)


def weight_grad_kept(core, gathered, dpre, offsets):
    width = dpre.shape[1]
    return pl.pallas_call(
        other_half_kernel,
        in_specs=[smem(), hbm(), vmem()],
        out_specs=vmem(),
        out_shape=jax.ShapeDtypeStruct((offsets, width // 2, width), BF16),
        scratch_shapes=[pltpu.VMEM(gathered.shape[1:], BF16), pltpu.SemaphoreType.DMA((3,))],
        compiler_params=params(16),
    )(core, gathered, dpre)


def widened(core, part, held):
    offsets, half, width = part.shape
    rest = [] if held is None else [held]
    return pl.pallas_call(
        own_rows_kernel if held is None else other_rows_kernel,
        in_specs=[smem(), vmem()] + [hbm()] * len(rest),
        out_specs=hbm(),
        out_shape=pltpu.HBM((offsets, 2 * half, width), F32),
        scratch_shapes=[pltpu.VMEM(part.shape, F32), pltpu.SemaphoreType.DMA((3,))],
        input_output_aliases={2: 0} if rest else {},
        compiler_params=params(16),
    )(core, part, *rest)


def pool_gradient(odd, near, dpre, weight):
    offsets, slots = near.shape
    groups = offsets // 3
    width = dpre.shape[1]
    rims = slots // 4

    def place(g, odd):
        b = lax.rem(g, 3)
        return (jnp.where(odd[0] == 1, b, 2 - b) * 3 + lax.div(g, 3), 0, 0)

    return pl.pallas_call(
        pool_grad_kernel,
        grid_spec=pltpu.PrefetchScalarGridSpec(
            num_scalar_prefetch=1,
            grid=(groups,),
            in_specs=[
                whole(near.shape),
                whole((slots, width)),
                pl.BlockSpec((3, width, width), lambda g, odd: (g, 0, 0)),
            ],
            out_specs=[whole((slots, width)), pl.BlockSpec((1, rims, width), place)],
        ),
        out_shape=[
            jax.ShapeDtypeStruct((slots, width), F32),
            jax.ShapeDtypeStruct((groups, rims, width), BF16),
        ],
        compiler_params=params(20),
    )(odd, near, dpre, weight)


def on_device(features, conv_weight, gamma, beta, cotangent, counts, rim_rows, neighbours):
    slots, width = features.shape
    rims = rim_rows.shape[0]
    offsets = neighbours.shape[0]
    groups = offsets // 3
    half = width // 2
    core = lax.axis_index("core").astype(jnp.int32)[None]
    odd_x = lax.rem(lax.axis_index(GX), 2).astype(jnp.int32)[None]
    odd_y = lax.rem(lax.axis_index(GY), 2).astype(jnp.int32)[None]
    rows = rim_rows.reshape(1, rims)
    rows, core, odd_x, odd_y = lax.optimization_barrier((rows, core, odd_x, odd_y))
    gamma_row = gamma.reshape(1, width)
    beta_row = beta.reshape(1, width)
    weight = pltpu.with_memory_space_constraint(conv_weight, pltpu.HBM)

    rim, feat_t, near = pl.pallas_call(
        rim_kernel,
        in_specs=[hbm()] * 3,
        out_specs=[vmem()] * 3,
        out_shape=[
            jax.ShapeDtypeStruct((rims, width), BF16),
            jax.ShapeDtypeStruct((width, slots), BF16),
            jax.ShapeDtypeStruct((offsets, slots), jnp.int32),
        ],
        scratch_shapes=[
            pltpu.VMEM((1, rims), jnp.int32),
            pltpu.VMEM((slots, width), BF16),
            pltpu.SemaphoreType.DMA((3,)),
        ],
        compiler_params=params(16),
    )(
        pltpu.with_memory_space_constraint(rows, pltpu.HBM),
        pltpu.with_memory_space_constraint(features, pltpu.HBM),
        pltpu.with_memory_space_constraint(neighbours, pltpu.HBM),
    )
    first, second = swaps(rim, rim, GX, 32)
    part, weight_t = forward_local(near, feat_t, weight)
    first, second, part, weight_t = lax.optimization_barrier((first, second, part, weight_t))
    column = pl.pallas_call(
        column_kernel,
        in_specs=[smem()] + [vmem()] * 3,
        out_specs=vmem(),
        out_shape=jax.ShapeDtypeStruct((3, rims, width), BF16),
        compiler_params=params(8),
    )(odd_x, rim, first, second)
    first, second = swaps(column, column, GY, 8)
    gathered, pre, stats = forward_rest(odd_y, near, column, first, second, part, weight_t)

    count_row = jnp.full((1, width), counts[0].astype(F32))
    sums = sums_over_all(jnp.concatenate([stats, count_row, jnp.zeros((1, width), F32)], axis=0))
    activated, dscaled, back = pl.pallas_call(
        activation_kernel,
        in_specs=[smem()] + [vmem()] * 5,
        out_shape=[
            jax.ShapeDtypeStruct((slots, width), BF16),
            jax.ShapeDtypeStruct((slots, width), F32),
            jax.ShapeDtypeStruct((2, width), F32),
        ],
        compiler_params=params(16),
    )(counts, pre, sums, gamma_row, beta_row, cotangent)
    back_sums = sums_over_all(back)

    gathered = pltpu.with_memory_space_constraint(gathered, pltpu.HBM)
    dpre, send, bn_grads = weight_grad_sent(
        core, counts, pre, dscaled, sums, gamma_row, back_sums, gathered, offsets
    )
    met = swapped(send)
    keep = weight_grad_kept(core, gathered, dpre, offsets)
    keep, met = lax.optimization_barrier((keep, met))
    mine = (keep.astype(F32) + met.astype(F32)).astype(BF16).reshape(offsets * half, width)

    plane_rows = offsets * half // 16
    depth_rows = -(-plane_rows // 64) * 8
    mine = exchange(mine.reshape(16, plane_rows, width), PLANE)
    local, partials = pool_gradient(odd_y, near, dpre, weight)
    gamma_grad, beta_grad = bn_grads[1], bn_grads[0]
    first, second = swaps(partials[:3], partials[6:], GY, 8)
    strip, first, second = pl.pallas_call(
        strip_kernel,
        in_specs=[smem()] + [vmem()] * 3,
        out_specs=[vmem()] * 3,
        out_shape=[
            jax.ShapeDtypeStruct((rims, width), F32),
            jax.ShapeDtypeStruct((rims, width), BF16),
            jax.ShapeDtypeStruct((rims, width), BF16),
        ],
        compiler_params=params(8),
    )(odd_x, partials, first, second)
    mine, local, strip, first, second, gamma_grad, beta_grad = lax.optimization_barrier(
        (mine, local, strip, first, second, gamma_grad, beta_grad)
    )
    mine = pl.pallas_call(
        plane_sum_kernel,
        in_specs=[hbm()],
        out_specs=vmem(),
        out_shape=jax.ShapeDtypeStruct((8 * depth_rows, width), BF16),
        scratch_shapes=[pltpu.VMEM((16, plane_rows, width), BF16), pltpu.SemaphoreType.DMA((4,))],
        compiler_params=params(16),
    )(pltpu.with_memory_space_constraint(mine, pltpu.HBM))
    mine = exchange(mine.reshape(8, depth_rows, width), DEPTH)
    mine = jnp.sum(mine.astype(F32), axis=0).astype(BF16)
    mine = shown(mine, DEPTH, 8).reshape(8 * depth_rows, width)[:plane_rows]
    mine, first, second = lax.optimization_barrier((mine, first, second))
    first, second = swaps(first, second, GX, 32)
    mine = shown(mine, PLANE, 16).reshape(offsets, half, width)
    input_grad = pl.pallas_call(
        input_grad_kernel,
        out_shape=jax.ShapeDtypeStruct((slots, width), BF16),
        compiler_params=params(16),
    )(rows, local, strip, first, second)
    mine, input_grad = lax.optimization_barrier((mine, input_grad))
    other = swapped(mine)
    held = widened(core, mine, None)
    other, held = lax.optimization_barrier((other, held))
    weight_grad = widened(core, other, held)
    return (activated, input_grad, weight_grad, gamma_grad, beta_grad)


def solution(mesh):
    finer = Mesh(mesh.devices.reshape(SIZES), AXES)
    return jax.shard_map(
        on_device,
        mesh=finer,
        in_specs=(P(AXES, None), P(), P(), P(), P(AXES, None), P(AXES), P(AXES), P(None, AXES)),
        out_specs=(P(AXES, None), P(AXES, None), P(), P(), P()),
        check_vma=False,
    )
```

```python
import functools

import jax
import jax.numpy as jnp
from jax import lax
from jax.experimental import pallas as pl
from jax.experimental.pallas import tpu as pltpu
from jax.sharding import Mesh, PartitionSpec as P

AXES = ("x", "zh", "y", "zl", "core")
SIZES = (4, 2, 4, 4, 2)
GX = ("x", "zh", "y")
GY = ("zl", "core")
PLANE = ("x", "y")
DEPTH = ("zh", "zl")
F32 = jnp.float32
BF16 = jnp.bfloat16


def params(mib):
    return pltpu.CompilerParams(vmem_limit_bytes=mib << 20)


def rows_of(first, second, dims):
    return lax.dot_general(first, second, (dims, ((), ())), preferred_element_type=F32)


def rim_kernel(rows_hbm, feat_hbm, near_hbm, rim_ref, feat_t_ref, near_ref, rows_ref, feat_ref, sem):
    copies = [
        pltpu.make_async_copy(rows_hbm, rows_ref, sem.at[0]),
        pltpu.make_async_copy(feat_hbm, feat_ref, sem.at[1]),
        pltpu.make_async_copy(near_hbm, near_ref, sem.at[2]),
    ]
    for copy in copies:
        copy.start()
    slots = feat_ref.shape[0]
    rims = rim_ref.shape[0]
    copies[0].wait()
    slot = lax.broadcasted_iota(jnp.int32, (slots, rims), 0)
    hit = jnp.where(slot == rows_ref[...], 1.0, 0.0).astype(BF16)
    copies[1].wait()
    feat = feat_ref[...]
    rim_ref[...] = rows_of(hit, feat, ((0,), (0,))).astype(BF16)
    feat_t_ref[...] = jnp.transpose(feat)
    copies[2].wait()


def local_kernel(near_ref, feat_t, weight_hbm, part_ref, weight_t_ref, held, sem):
    groups = near_ref.shape[0] // 3
    width, slots = feat_t.shape
    half = width // 2
    offsets = 3 * groups
    copies = [
        pltpu.make_async_copy(
            weight_hbm.at[pl.ds(9 * i, 9)], held.at[pl.ds(9 * i, 9)], sem.at[i]
        )
        for i in range(groups // 3)
    ]
    for copy in copies:
        copy.start()
    slot = lax.broadcasted_iota(jnp.int32, (slots, slots), 0)

    def gather(g, carry):
        hits = [
            jnp.where(slot == near_ref[pl.ds(3 * g + j, 1), :], 1.0, 0.0).astype(BF16) for j in range(3)
        ]
        rows = jnp.dot(feat_t[...], jnp.concatenate(hits, axis=1), preferred_element_type=F32).astype(BF16)
        for j in range(3):
            at = pl.ds(pl.multiple_of((3 * g + j) * half, half), half)
            part_ref[0, at, :] = rows[:half, j * slots : (j + 1) * slots]
            part_ref[1, at, :] = rows[half:, j * slots : (j + 1) * slots]
        return carry

    lax.fori_loop(0, groups, gather, 0, unroll=True)
    for copy in copies:
        copy.wait()

    def turn(k, carry):
        for h in range(2):
            at = pl.ds(pl.multiple_of((h * offsets + k) * half, half), half)
            weight_t_ref[:, at] = jnp.transpose(held[k, h * half : (h + 1) * half, :])
        return carry

    lax.fori_loop(0, offsets, turn, 0, unroll=3)


def column_kernel(odd_ref, rim_ref, first_ref, second_ref, column_ref):
    column_ref[1] = rim_ref[...]

    @pl.when(odd_ref[0] == 1)
    def _():
        column_ref[0] = first_ref[...]
        column_ref[2] = second_ref[...]

    @pl.when(odd_ref[0] == 0)
    def _():
        column_ref[0] = second_ref[...]
        column_ref[2] = first_ref[...]


def forward_kernel(
    odd_ref, near_ref, column_ref, first_ref, second_ref, part_ref, weight_t_ref, whole_rows, pre_ref, stats_ref, halo_ref
):
    groups, rims, width = halo_ref.shape
    for a in range(3):
        halo_ref[3 * a + 1] = column_ref[a]

    @pl.when(odd_ref[0] == 1)
    def _():
        for a in range(3):
            halo_ref[3 * a] = first_ref[a]
            halo_ref[3 * a + 2] = second_ref[a]

    @pl.when(odd_ref[0] == 0)
    def _():
        for a in range(3):
            halo_ref[3 * a] = second_ref[a]
            halo_ref[3 * a + 2] = first_ref[a]

    slots = near_ref.shape[1]
    half = width // 2
    offsets = 3 * groups
    slot = lax.broadcasted_iota(jnp.int32, (rims, slots), 0) + slots
    def gather(g, carry):
        halo_t = jnp.transpose(halo_ref[g])
        hits = [
            jnp.where(slot + g * rims == near_ref[pl.ds(3 * g + j, 1), :], 1.0, 0.0).astype(BF16)
            for j in range(3)
        ]
        rows = jnp.dot(halo_t, jnp.concatenate(hits, axis=1), preferred_element_type=F32).astype(BF16)
        for j in range(3):
            at = pl.ds(pl.multiple_of((3 * g + j) * half, half), half)
            for h in range(2):
                found = rows[h * half : (h + 1) * half, j * slots : (j + 1) * slots]
                whole_rows[h, at, :] = part_ref[h, at, :] + found
        return carry

    lax.fori_loop(0, groups, gather, 0, unroll=True)
    pre_t = None
    for h in range(2):
        weight_t = weight_t_ref[:, h * offsets * half : (h + 1) * offsets * half]
        term = jnp.dot(weight_t, whole_rows[h], preferred_element_type=F32)
        pre_t = term if pre_t is None else pre_t + term
    pre = jnp.transpose(pre_t)
    pre_ref[...] = pre
    stats_ref[0:1, :] = jnp.sum(pre, axis=0, keepdims=True)
    stats_ref[1:2, :] = jnp.sum(pre * pre, axis=0, keepdims=True)


def moments(sums_ref):
    sums = jnp.sum(sums_ref[...], axis=0)
    total = sums[2:3, :]
    average = sums[0:1, :] / total
    variance = sums[1:2, :] / total - average * average
    return average, 1.0 / jnp.sqrt(variance + 1e-05), total


def activation_kernel(
    count_ref, pre_ref, sums_ref, gamma_ref, beta_ref, cotangent_ref, active_ref, dscaled_ref, stats_ref
):
    slots = pre_ref.shape[0]
    average, inv_std, _ = moments(sums_ref)
    centered = (pre_ref[...] - average) * inv_std
    scaled = gamma_ref[...] * centered + beta_ref[...]
    sig = jax.nn.sigmoid(scaled)
    mask = lax.broadcasted_iota(jnp.int32, pre_ref.shape, 0) < count_ref[0]
    active_ref[...] = jnp.where(mask, scaled * sig, 0.0).astype(BF16)
    dscaled = jnp.where(mask, cotangent_ref[...].astype(F32) * sig * (1.0 + scaled * (1.0 - sig)), 0.0)
    dscaled_ref[...] = dscaled
    stats_ref[0:1, :] = jnp.sum(dscaled, axis=0, keepdims=True)
    stats_ref[1:2, :] = jnp.sum(dscaled * centered, axis=0, keepdims=True)


def half_products(gathered_ref, which, dpre, out_ref):
    span = gathered_ref.shape[1] // 3
    half = out_ref.shape[1]
    for i in range(3):
        held = gathered_ref[which, i * span : (i + 1) * span, :]
        term = jnp.dot(held, dpre, preferred_element_type=F32)
        out_ref[i * (span // half) : (i + 1) * (span // half)] = term.astype(BF16).reshape(
            span // half, half, out_ref.shape[2]
        )


def weight_grad_kernel(
    half_ref, count_ref, pre_ref, dscaled_ref, sums_ref, gamma_ref, back_ref, gathered_ref, dpre_ref, send_ref, bn_ref
):
    average, inv_std, total = moments(sums_ref)
    back = jnp.sum(back_ref[...], axis=0)
    bn_ref[...] = back
    centered = (pre_ref[...] - average) * inv_std
    grad = gamma_ref[...] * inv_std * (dscaled_ref[...] - (back[0:1, :] + centered * back[1:2, :]) / total)
    mask = lax.broadcasted_iota(jnp.int32, pre_ref.shape, 0) < count_ref[0]
    dpre = jnp.where(mask, grad, 0.0).astype(BF16)
    dpre_ref[...] = dpre
    half_products(gathered_ref, 1 - half_ref[0], dpre, send_ref)


def other_half_kernel(half_ref, gathered_ref, dpre_ref, keep_ref):
    half_products(gathered_ref, half_ref[0], dpre_ref[...], keep_ref)


def pool_grad_kernel(odd_ref, near_ref, dpre_ref, weight_ref, local_ref, halo_ref):
    step = pl.program_id(0)
    slots, width = dpre_ref.shape
    rims = halo_ref.shape[1]
    pool_rows = slots + rims
    slot = lax.broadcasted_iota(jnp.int32, (pool_rows, slots), 0)
    hits, contribs = [], []
    for j in range(3):
        row = near_ref[pl.ds(3 * step + j, 1), :]
        row = jnp.where(row >= slots, row - step * rims, row)
        hits.append(jnp.where(slot == row, 1.0, 0.0).astype(BF16))
        contribs.append(rows_of(dpre_ref[...], weight_ref[j], ((1,), (1,))).astype(BF16))
    total = jnp.dot(
        jnp.concatenate(hits, axis=1), jnp.concatenate(contribs, axis=0), preferred_element_type=F32
    )
    halo_ref[0] = total[slots:, :].astype(BF16)

    @pl.when(step == 0)
    def _():
        local_ref[...] = total[:slots, :]

    @pl.when(step > 0)
    def _():
        local_ref[...] += total[:slots, :]


def strip_kernel(odd_ref, parts_ref, first_ref, second_ref, strip_ref, out_first_ref, out_second_ref):
    strips = [
        parts_ref[3 + a].astype(F32) + first_ref[a].astype(F32) + second_ref[a].astype(F32)
        for a in range(3)
    ]
    strip_ref[...] = strips[1]
    odd = odd_ref[0] == 1
    out_first_ref[...] = jnp.where(odd, strips[0], strips[2]).astype(BF16)
    out_second_ref[...] = jnp.where(odd, strips[2], strips[0]).astype(BF16)


def input_grad_kernel(rows_ref, local_ref, strip_ref, first_ref, second_ref, out_ref):
    slots = local_ref.shape[0]
    rims = strip_ref.shape[0]
    slot = lax.broadcasted_iota(jnp.int32, (slots, rims), 0)
    hit = jnp.where(slot == rows_ref[...], 1.0, 0.0).astype(BF16)
    final = strip_ref[...] + first_ref[...].astype(F32) + second_ref[...].astype(F32)
    high = final.astype(BF16)
    low = (final - high.astype(F32)).astype(BF16)
    added = jnp.dot(hit, high, preferred_element_type=F32) + jnp.dot(hit, low, preferred_element_type=F32)
    out_ref[...] = (local_ref[...] + added).astype(BF16)


def spread_sum_kernel(parts_ref, out_ref):
    out_ref[...] = jnp.broadcast_to(jnp.sum(parts_ref[...], axis=0, keepdims=True), out_ref.shape)


def plane_sum_kernel(parts_ref, out_ref):
    rows = parts_ref.shape[1]
    out_ref[rows:, :] = jnp.zeros((out_ref.shape[0] - rows, out_ref.shape[1]), BF16)
    out_ref[:rows, :] = jnp.sum(parts_ref[...].astype(F32), axis=0).astype(BF16)


def met_kernel(keep_ref, met_ref, out_hbm, total, sem):
    span = total.shape[0] // 3
    copies = []
    for n in range(3):
        at = pl.ds(n * span, span)
        total[at] = (keep_ref[at].astype(F32) + met_ref[at].astype(F32)).astype(BF16)
        copies.append(pltpu.make_async_copy(total.at[at], out_hbm.at[at], sem.at[n]))
        copies[-1].start()
    for copy in copies:
        copy.wait()


def repeat_kernel(part_ref, out_hbm, sem):
    count, rows, _ = out_hbm.shape
    copies = [
        pltpu.make_async_copy(part_ref.at[pl.ds(0, rows)], out_hbm.at[n], sem.at[n]) for n in range(count)
    ]
    for copy in copies:
        copy.start()
    for copy in copies:
        copy.wait()


def put_rows(part_ref, place, out_hbm, wide, sem):
    half = part_ref.shape[1]
    count = part_ref.shape[0] // 3
    rows = pl.ds(pl.multiple_of(place * half, half), half)
    copies = []
    for n in range(3):
        at = pl.ds(n * count, count)
        wide[at] = part_ref[at].astype(F32)
        copies.append(pltpu.make_async_copy(wide.at[at], out_hbm.at[at, rows], sem.at[n]))
        copies[-1].start()
    for copy in copies:
        copy.wait()


def own_rows_kernel(half_ref, part_ref, out_hbm, wide, sem):
    put_rows(part_ref, half_ref[0], out_hbm, wide, sem)


def other_rows_kernel(half_ref, part_ref, held_hbm, out_hbm, wide, sem):
    put_rows(part_ref, 1 - half_ref[0], out_hbm, wide, sem)


def smem():
    return pl.BlockSpec(memory_space=pltpu.SMEM)


def whole(shape):
    return pl.BlockSpec(shape, lambda *_: (0,) * len(shape))


def swaps(first, second, axes, count):
    met = []
    for value, start in ((first, 0), (second, 1)):
        edges = [(i, i + 1) for i in range(start, count - 1, 2)]
        met.append(lax.ppermute(value, axes, edges + [(j, i) for i, j in edges]))
    return met


def exchange(parts, axes):
    return lax.all_to_all(parts, axes, 0, 0)


def shown(part, axes, count):
    return exchange(jnp.broadcast_to(part[None], (count,) + part.shape), axes)


def sums_over_all(part):
    inner = shown(part, ("zh", "zl", "core"), 16)
    spread = pl.pallas_call(
        spread_sum_kernel,
        in_specs=[vmem()],
        out_specs=vmem(),
        out_shape=jax.ShapeDtypeStruct(inner.shape, F32),
        compiler_params=params(4),
    )(inner)
    return exchange(spread, PLANE)


def vmem():
    return pl.BlockSpec(memory_space=pltpu.VMEM)


def hbm():
    return pl.BlockSpec(memory_space=pl.ANY)


def swapped(value):
    return lax.ppermute(value, "core", [(0, 1), (1, 0)])


def forward_local(near, feat_t, weight):
    offsets, slots = near.shape
    width = feat_t.shape[0]
    return pl.pallas_call(
        local_kernel,
        in_specs=[vmem(), vmem(), hbm()],
        out_specs=[vmem(), vmem()],
        out_shape=[
            jax.ShapeDtypeStruct((2, offsets * width // 2, slots), BF16),
            jax.ShapeDtypeStruct((width, offsets * width), BF16),
        ],
        scratch_shapes=[pltpu.VMEM((offsets, width, width), BF16), pltpu.SemaphoreType.DMA((3,))],
        compiler_params=params(24),
    )(near, feat_t, weight)


def forward_rest(odd, near, column, first, second, part, weight_t):
    offsets, slots = near.shape
    _, rims, width = column.shape
    groups = offsets // 3
    return pl.pallas_call(
        forward_kernel,
        in_specs=[smem()] + [vmem()] * 6,
        out_specs=[vmem()] * 3,
        out_shape=[
            jax.ShapeDtypeStruct(part.shape, BF16),
            jax.ShapeDtypeStruct((slots, width), F32),
            jax.ShapeDtypeStruct((2, width), F32),
        ],
        scratch_shapes=[
            pltpu.VMEM((groups, rims, width), BF16),
        ],
        compiler_params=params(24),
    )(odd, near, column, first, second, part, weight_t)


def weight_grad_sent(core, counts, pre, dscaled, sums, gamma_row, back_sums, gathered, offsets):
    slots, width = pre.shape
    return pl.pallas_call(
        weight_grad_kernel,
        in_specs=[smem(), smem()] + [vmem()] * 6,
        out_specs=[vmem()] * 3,
        out_shape=[
            jax.ShapeDtypeStruct((slots, width), BF16),
            jax.ShapeDtypeStruct((offsets, width // 2, width), BF16),
            jax.ShapeDtypeStruct((2, width), F32),
        ],
        compiler_params=params(16),
    )(core, counts, pre, dscaled, sums, gamma_row, back_sums, gathered)


def weight_grad_kept(core, gathered, dpre, offsets):
    width = dpre.shape[1]
    return pl.pallas_call(
        other_half_kernel,
        in_specs=[smem(), vmem(), vmem()],
        out_specs=vmem(),
        out_shape=jax.ShapeDtypeStruct((offsets, width // 2, width), BF16),
        compiler_params=params(16),
    )(core, gathered, dpre)


def widened(core, part, held):
    offsets, half, width = part.shape
    rest = [] if held is None else [held]
    return pl.pallas_call(
        own_rows_kernel if held is None else other_rows_kernel,
        in_specs=[smem(), vmem()] + [hbm()] * len(rest),
        out_specs=hbm(),
        out_shape=pltpu.HBM((offsets, 2 * half, width), F32),
        scratch_shapes=[pltpu.VMEM(part.shape, F32), pltpu.SemaphoreType.DMA((3,))],
        input_output_aliases={2: 0} if rest else {},
        compiler_params=params(16),
    )(core, part, *rest)


def pool_gradient(odd, near, dpre, weight):
    offsets, slots = near.shape
    groups = offsets // 3
    width = dpre.shape[1]
    rims = slots // 4

    def place(g, odd):
        b = lax.rem(g, 3)
        return (jnp.where(odd[0] == 1, b, 2 - b) * 3 + lax.div(g, 3), 0, 0)

    return pl.pallas_call(
        pool_grad_kernel,
        grid_spec=pltpu.PrefetchScalarGridSpec(
            num_scalar_prefetch=1,
            grid=(groups,),
            in_specs=[
                whole(near.shape),
                whole((slots, width)),
                pl.BlockSpec((3, width, width), lambda g, odd: (g, 0, 0)),
            ],
            out_specs=[whole((slots, width)), pl.BlockSpec((1, rims, width), place)],
        ),
        out_shape=[
            jax.ShapeDtypeStruct((slots, width), F32),
            jax.ShapeDtypeStruct((groups, rims, width), BF16),
        ],
        compiler_params=params(20),
    )(odd, near, dpre, weight)


def on_device(features, conv_weight, gamma, beta, cotangent, counts, rim_rows, neighbours):
    slots, width = features.shape
    rims = rim_rows.shape[0]
    offsets = neighbours.shape[0]
    groups = offsets // 3
    half = width // 2
    core = lax.axis_index("core").astype(jnp.int32)[None]
    odd_x = lax.rem(lax.axis_index(GX), 2).astype(jnp.int32)[None]
    odd_y = lax.rem(lax.axis_index(GY), 2).astype(jnp.int32)[None]
    rows = rim_rows.reshape(1, rims)
    rows, core, odd_x, odd_y = lax.optimization_barrier((rows, core, odd_x, odd_y))
    gamma_row = gamma.reshape(1, width)
    beta_row = beta.reshape(1, width)
    weight = pltpu.with_memory_space_constraint(conv_weight, pltpu.HBM)

    rim, feat_t, near = pl.pallas_call(
        rim_kernel,
        in_specs=[hbm()] * 3,
        out_specs=[vmem()] * 3,
        out_shape=[
            jax.ShapeDtypeStruct((rims, width), BF16),
            jax.ShapeDtypeStruct((width, slots), BF16),
            jax.ShapeDtypeStruct((offsets, slots), jnp.int32),
        ],
        scratch_shapes=[
            pltpu.VMEM((1, rims), jnp.int32),
            pltpu.VMEM((slots, width), BF16),
            pltpu.SemaphoreType.DMA((3,)),
        ],
        compiler_params=params(16),
    )(
        pltpu.with_memory_space_constraint(rows, pltpu.HBM),
        pltpu.with_memory_space_constraint(features, pltpu.HBM),
        pltpu.with_memory_space_constraint(neighbours, pltpu.HBM),
    )
    first, second = swaps(rim, rim, GX, 32)
    part, weight_t = forward_local(near, feat_t, weight)
    first, second, part, weight_t = lax.optimization_barrier((first, second, part, weight_t))
    column = pl.pallas_call(
        column_kernel,
        in_specs=[smem()] + [vmem()] * 3,
        out_specs=vmem(),
        out_shape=jax.ShapeDtypeStruct((3, rims, width), BF16),
        compiler_params=params(8),
    )(odd_x, rim, first, second)
    first, second = swaps(column, column, GY, 8)
    gathered, pre, stats = forward_rest(odd_y, near, column, first, second, part, weight_t)

    count_row = jnp.full((1, width), counts[0].astype(F32))
    sums = sums_over_all(jnp.concatenate([stats, count_row, jnp.zeros((1, width), F32)], axis=0))
    activated, dscaled, back = pl.pallas_call(
        activation_kernel,
        in_specs=[smem()] + [vmem()] * 5,
        out_shape=[
            jax.ShapeDtypeStruct((slots, width), BF16),
            jax.ShapeDtypeStruct((slots, width), F32),
            jax.ShapeDtypeStruct((2, width), F32),
        ],
        compiler_params=params(16),
    )(counts, pre, sums, gamma_row, beta_row, cotangent)
    back_sums = sums_over_all(back)

    dpre, send, bn_grads = weight_grad_sent(
        core, counts, pre, dscaled, sums, gamma_row, back_sums, gathered, offsets
    )
    met = swapped(send)
    keep = weight_grad_kept(core, gathered, dpre, offsets)
    mine = pl.pallas_call(
        met_kernel,
        in_specs=[vmem()] * 2,
        out_specs=hbm(),
        out_shape=pltpu.HBM(keep.shape, BF16),
        scratch_shapes=[pltpu.VMEM(keep.shape, BF16), pltpu.SemaphoreType.DMA((3,))],
        compiler_params=params(8),
    )(keep, met)

    plane_rows = offsets * half // 16
    depth_rows = -(-plane_rows // 64) * 8
    mine = exchange(mine.reshape(16, plane_rows, width), PLANE)
    local, partials = pool_gradient(odd_y, near, dpre, weight)
    gamma_grad, beta_grad = bn_grads[1], bn_grads[0]
    first, second = swaps(partials[:3], partials[6:], GY, 8)
    strip, first, second = pl.pallas_call(
        strip_kernel,
        in_specs=[smem()] + [vmem()] * 3,
        out_specs=[vmem()] * 3,
        out_shape=[
            jax.ShapeDtypeStruct((rims, width), F32),
            jax.ShapeDtypeStruct((rims, width), BF16),
            jax.ShapeDtypeStruct((rims, width), BF16),
        ],
        compiler_params=params(8),
    )(odd_x, partials, first, second)
    mine, local, strip, first, second, gamma_grad, beta_grad = lax.optimization_barrier(
        (mine, local, strip, first, second, gamma_grad, beta_grad)
    )
    mine = pl.pallas_call(
        plane_sum_kernel,
        in_specs=[vmem()],
        out_specs=vmem(),
        out_shape=jax.ShapeDtypeStruct((8 * depth_rows, width), BF16),
        compiler_params=params(8),
    )(mine)
    mine = exchange(mine.reshape(8, depth_rows, width), DEPTH)
    mine = jnp.sum(mine.astype(F32), axis=0).astype(BF16)
    mine = shown(mine, DEPTH, 8).reshape(8 * depth_rows, width)
    mine, first, second = lax.optimization_barrier((mine, first, second))
    first, second = swaps(first, second, GX, 32)
    mine = pl.pallas_call(
        repeat_kernel,
        in_specs=[vmem()],
        out_specs=hbm(),
        out_shape=pltpu.HBM((16, plane_rows, width), BF16),
        scratch_shapes=[pltpu.SemaphoreType.DMA((16,))],
        compiler_params=params(8),
    )(mine)
    mine = exchange(mine, PLANE).reshape(offsets, half, width)
    input_grad = pl.pallas_call(
        input_grad_kernel,
        out_shape=jax.ShapeDtypeStruct((slots, width), BF16),
        compiler_params=params(16),
    )(rows, local, strip, first, second)
    mine, input_grad = lax.optimization_barrier((mine, input_grad))
    other = swapped(mine)
    held = widened(core, mine, None)
    other, held = lax.optimization_barrier((other, held))
    weight_grad = widened(core, other, held)
    return (activated, input_grad, weight_grad, gamma_grad, beta_grad)


def solution(mesh):
    finer = Mesh(mesh.devices.reshape(SIZES), AXES)
    return jax.shard_map(
        on_device,
        mesh=finer,
        in_specs=(P(AXES, None), P(), P(), P(), P(AXES, None), P(AXES), P(AXES), P(None, AXES)),
        out_specs=(P(AXES, None), P(AXES, None), P(), P(), P()),
        check_vma=False,
    )
```

```python
import functools

import jax
import jax.numpy as jnp
from jax import lax
from jax.experimental import pallas as pl
from jax.experimental.pallas import tpu as pltpu
from jax.sharding import Mesh, PartitionSpec as P

AXES = ("x", "zh", "y", "zl", "core")
SIZES = (4, 2, 4, 4, 2)
GX = ("x", "zh", "y")
GY = ("zl", "core")
PLANE = ("x", "y")
DEPTH = ("zh", "zl")
F32 = jnp.float32
BF16 = jnp.bfloat16


def params(mib):
    return pltpu.CompilerParams(vmem_limit_bytes=mib << 20)


def rows_of(first, second, dims):
    return lax.dot_general(first, second, (dims, ((), ())), preferred_element_type=F32)


def rim_kernel(rows_hbm, feat_hbm, near_hbm, rim_ref, feat_t_ref, near_ref, rows_ref, feat_ref, sem):
    copies = [
        pltpu.make_async_copy(rows_hbm, rows_ref, sem.at[0]),
        pltpu.make_async_copy(feat_hbm, feat_ref, sem.at[1]),
        pltpu.make_async_copy(near_hbm, near_ref, sem.at[2]),
    ]
    for copy in copies:
        copy.start()
    slots = feat_ref.shape[0]
    rims = rim_ref.shape[0]
    copies[0].wait()
    slot = lax.broadcasted_iota(jnp.int32, (slots, rims), 0)
    hit = jnp.where(slot == rows_ref[...], 1.0, 0.0).astype(BF16)
    copies[1].wait()
    feat = feat_ref[...]
    rim_ref[...] = rows_of(hit, feat, ((0,), (0,))).astype(BF16)
    feat_t_ref[...] = jnp.transpose(feat)
    copies[2].wait()


def order_of(groups):
    return sorted(range(groups), key=lambda g: g % 3 != 1)


def local_kernel(near_ref, feat_t, weight_hbm, mid_ref, rest_ref, mid_weight_ref, rest_weight_ref, held, sem):
    groups = near_ref.shape[0] // 3
    width, slots = feat_t.shape
    half = width // 2
    copies = [
        pltpu.make_async_copy(
            weight_hbm.at[pl.ds(9 * i, 9)], held.at[pl.ds(9 * i, 9)], sem.at[i]
        )
        for i in range(groups // 3)
    ]
    for copy in copies:
        copy.start()
    slot = lax.broadcasted_iota(jnp.int32, (slots, slots), 0)
    for place, g in enumerate(order_of(groups)):
        part_ref, first = (mid_ref, 0) if place < 3 else (rest_ref, 9)
        hits = [
            jnp.where(slot == near_ref[3 * g + j : 3 * g + j + 1, :], 1.0, 0.0).astype(BF16) for j in range(3)
        ]
        rows = jnp.dot(feat_t[...], jnp.concatenate(hits, axis=1), preferred_element_type=F32).astype(BF16)
        for j in range(3):
            at = (3 * place + j - first) * half
            part_ref[0, at : at + half, :] = rows[:half, j * slots : (j + 1) * slots]
            part_ref[1, at : at + half, :] = rows[half:, j * slots : (j + 1) * slots]
    for copy in copies:
        copy.wait()
    for place, g in enumerate(order_of(groups)):
        out_ref, first = (mid_weight_ref, 0) if place < 3 else (rest_weight_ref, 9)
        count = out_ref.shape[1] // width
        for j in range(3):
            for h in range(2):
                at = (h * count + 3 * place + j - first) * half
                out_ref[:, at : at + half] = jnp.transpose(held[3 * g + j, h * half : (h + 1) * half, :])


def add_rim(near_ref, g, rim, part_ref, rows_ref, first):
    rims, width = rim.shape
    slots = near_ref.shape[1]
    half = width // 2
    slot = lax.broadcasted_iota(jnp.int32, (rims, slots), 0) + (slots + g * rims)
    hits = [
        jnp.where(slot == near_ref[3 * g + j : 3 * g + j + 1, :], 1.0, 0.0).astype(BF16) for j in range(3)
    ]
    rows = jnp.dot(jnp.transpose(rim), jnp.concatenate(hits, axis=1), preferred_element_type=F32).astype(BF16)
    for j in range(3):
        at = (first + j) * half
        for h in range(2):
            found = rows[h * half : (h + 1) * half, j * slots : (j + 1) * slots]
            rows_ref[h, at : at + half, :] = part_ref[h, at : at + half, :] + found


def products_t(weight_t_ref, rows_ref):
    span = weight_t_ref.shape[1] // 2
    return sum(
        jnp.dot(weight_t_ref[:, h * span : (h + 1) * span], rows_ref[h], preferred_element_type=F32)
        for h in range(2)
    )


def middle_kernel(near_ref, column_ref, part_ref, weight_t_ref, rows_ref, pre_t_ref):
    groups = near_ref.shape[0] // 3
    span = part_ref.shape[1] // 3
    for place, g in enumerate(order_of(groups)[:3]):
        if g == groups // 2:
            at = slice(place * span, (place + 1) * span)
            rows_ref[:, at, :] = part_ref[:, at, :]
        else:
            add_rim(near_ref, g, column_ref[g // 3], part_ref, rows_ref, 3 * place)
    pre_t_ref[...] = products_t(weight_t_ref, rows_ref)


def column_kernel(odd_ref, rim_ref, first_ref, second_ref, column_ref):
    column_ref[1] = rim_ref[...]

    @pl.when(odd_ref[0] == 1)
    def _():
        column_ref[0] = first_ref[...]
        column_ref[2] = second_ref[...]

    @pl.when(odd_ref[0] == 0)
    def _():
        column_ref[0] = second_ref[...]
        column_ref[2] = first_ref[...]


def forward_kernel(
    odd_ref, near_ref, first_ref, second_ref, part_ref, weight_t_ref, pre_t_ref, rows_ref, pre_ref, stats_ref, sides
):
    groups = near_ref.shape[0] // 3

    @pl.when(odd_ref[0] == 1)
    def _():
        sides[0] = first_ref[...]
        sides[1] = second_ref[...]

    @pl.when(odd_ref[0] == 0)
    def _():
        sides[0] = second_ref[...]
        sides[1] = first_ref[...]

    for place, g in enumerate(order_of(groups)[3:]):
        add_rim(near_ref, g, sides[g % 3 // 2, g // 3], part_ref, rows_ref, 3 * place)
    pre = jnp.transpose(pre_t_ref[...] + products_t(weight_t_ref, rows_ref))
    pre_ref[...] = pre
    stats_ref[0:1, :] = jnp.sum(pre, axis=0, keepdims=True)
    stats_ref[1:2, :] = jnp.sum(pre * pre, axis=0, keepdims=True)


def moments(sums_ref):
    sums = jnp.sum(sums_ref[...], axis=0)
    total = sums[2:3, :]
    average = sums[0:1, :] / total
    variance = sums[1:2, :] / total - average * average
    return average, 1.0 / jnp.sqrt(variance + 1e-05), total


def activation_kernel(
    count_ref, pre_ref, sums_ref, gamma_ref, beta_ref, cotangent_ref, active_ref, dscaled_ref, stats_ref
):
    slots = pre_ref.shape[0]
    average, inv_std, _ = moments(sums_ref)
    centered = (pre_ref[...] - average) * inv_std
    scaled = gamma_ref[...] * centered + beta_ref[...]
    sig = jax.nn.sigmoid(scaled)
    mask = lax.broadcasted_iota(jnp.int32, pre_ref.shape, 0) < count_ref[0]
    active_ref[...] = jnp.where(mask, scaled * sig, 0.0).astype(BF16)
    dscaled = jnp.where(mask, cotangent_ref[...].astype(F32) * sig * (1.0 + scaled * (1.0 - sig)), 0.0)
    dscaled_ref[...] = dscaled
    stats_ref[0:1, :] = jnp.sum(dscaled, axis=0, keepdims=True)
    stats_ref[1:2, :] = jnp.sum(dscaled * centered, axis=0, keepdims=True)


def half_products(mid_ref, rest_ref, which, dpre, out_ref):
    span = mid_ref.shape[1]
    half = out_ref.shape[1]
    for i in range(3):
        held = mid_ref[which] if i == 0 else rest_ref[which, (i - 1) * span : i * span, :]
        term = jnp.dot(held, dpre, preferred_element_type=F32)
        out_ref[i * (span // half) : (i + 1) * (span // half)] = term.astype(BF16).reshape(
            span // half, half, out_ref.shape[2]
        )


def weight_grad_kernel(
    half_ref, count_ref, pre_ref, dscaled_ref, sums_ref, gamma_ref, back_ref, mid_ref, rest_ref, dpre_ref, send_ref, bn_ref
):
    average, inv_std, total = moments(sums_ref)
    back = jnp.sum(back_ref[...], axis=0)
    bn_ref[...] = back
    centered = (pre_ref[...] - average) * inv_std
    grad = gamma_ref[...] * inv_std * (dscaled_ref[...] - (back[0:1, :] + centered * back[1:2, :]) / total)
    mask = lax.broadcasted_iota(jnp.int32, pre_ref.shape, 0) < count_ref[0]
    dpre = jnp.where(mask, grad, 0.0).astype(BF16)
    dpre_ref[...] = dpre
    half_products(mid_ref, rest_ref, 1 - half_ref[0], dpre, send_ref)


def other_half_kernel(half_ref, mid_ref, rest_ref, dpre_ref, keep_ref):
    half_products(mid_ref, rest_ref, half_ref[0], dpre_ref[...], keep_ref)


def pool_grad_kernel(odd_ref, near_ref, dpre_ref, weight_ref, local_ref, halo_ref):
    step = pl.program_id(0)
    slots, width = dpre_ref.shape
    rims = halo_ref.shape[1]
    pool_rows = slots + rims
    slot = lax.broadcasted_iota(jnp.int32, (pool_rows, slots), 0)
    hits, contribs = [], []
    for j in range(3):
        row = near_ref[pl.ds(3 * step + j, 1), :]
        row = jnp.where(row >= slots, row - step * rims, row)
        hits.append(jnp.where(slot == row, 1.0, 0.0).astype(BF16))
        contribs.append(rows_of(dpre_ref[...], weight_ref[j], ((1,), (1,))).astype(BF16))
    total = jnp.dot(
        jnp.concatenate(hits, axis=1), jnp.concatenate(contribs, axis=0), preferred_element_type=F32
    )
    halo_ref[0] = total[slots:, :].astype(BF16)

    @pl.when(step == 0)
    def _():
        local_ref[...] = total[:slots, :]

    @pl.when(step > 0)
    def _():
        local_ref[...] += total[:slots, :]


def strip_kernel(odd_ref, parts_ref, first_ref, second_ref, strip_ref, out_first_ref, out_second_ref):
    strips = [
        parts_ref[3 + a].astype(F32) + first_ref[a].astype(F32) + second_ref[a].astype(F32)
        for a in range(3)
    ]
    strip_ref[...] = strips[1]
    odd = odd_ref[0] == 1
    out_first_ref[...] = jnp.where(odd, strips[0], strips[2]).astype(BF16)
    out_second_ref[...] = jnp.where(odd, strips[2], strips[0]).astype(BF16)


def input_grad_kernel(rows_ref, local_ref, strip_ref, first_ref, second_ref, out_ref):
    slots = local_ref.shape[0]
    rims = strip_ref.shape[0]
    slot = lax.broadcasted_iota(jnp.int32, (slots, rims), 0)
    hit = jnp.where(slot == rows_ref[...], 1.0, 0.0).astype(BF16)
    final = strip_ref[...] + first_ref[...].astype(F32) + second_ref[...].astype(F32)
    high = final.astype(BF16)
    low = (final - high.astype(F32)).astype(BF16)
    added = jnp.dot(hit, high, preferred_element_type=F32) + jnp.dot(hit, low, preferred_element_type=F32)
    out_ref[...] = (local_ref[...] + added).astype(BF16)


def spread_sum_kernel(parts_ref, out_ref):
    out_ref[...] = jnp.broadcast_to(jnp.sum(parts_ref[...], axis=0, keepdims=True), out_ref.shape)


def plane_sum_kernel(parts_ref, out_ref):
    rows = parts_ref.shape[1]
    out_ref[rows:, :] = jnp.zeros((out_ref.shape[0] - rows, out_ref.shape[1]), BF16)
    out_ref[:rows, :] = jnp.sum(parts_ref[...].astype(F32), axis=0).astype(BF16)


def met_kernel(keep_ref, met_ref, out_hbm, total, sem):
    span = total.shape[0] // 3
    copies = []
    for n in range(3):
        at = pl.ds(n * span, span)
        total[at] = (keep_ref[at].astype(F32) + met_ref[at].astype(F32)).astype(BF16)
        copies.append(pltpu.make_async_copy(total.at[at], out_hbm.at[at], sem.at[n]))
        copies[-1].start()
    for copy in copies:
        copy.wait()


def repeat_kernel(part_ref, out_hbm, sem):
    count, rows, _ = out_hbm.shape
    copies = [
        pltpu.make_async_copy(part_ref.at[pl.ds(0, rows)], out_hbm.at[n], sem.at[n]) for n in range(count)
    ]
    for copy in copies:
        copy.start()
    for copy in copies:
        copy.wait()


def put_rows(part_ref, place, out_hbm, wide, sem):
    half = part_ref.shape[1]
    rows = pl.ds(pl.multiple_of(place * half, half), half)
    copies = []
    for n, g in enumerate(order_of(part_ref.shape[0] // 3)):
        at = pl.ds(3 * n, 3)
        wide[at] = part_ref[at].astype(F32)
        copies.append(pltpu.make_async_copy(wide.at[at], out_hbm.at[pl.ds(3 * g, 3), rows], sem.at[n]))
        copies[-1].start()
    for copy in copies:
        copy.wait()


def own_rows_kernel(half_ref, part_ref, out_hbm, wide, sem):
    put_rows(part_ref, half_ref[0], out_hbm, wide, sem)


def other_rows_kernel(half_ref, part_ref, held_hbm, out_hbm, wide, sem):
    put_rows(part_ref, 1 - half_ref[0], out_hbm, wide, sem)


def smem():
    return pl.BlockSpec(memory_space=pltpu.SMEM)


def whole(shape):
    return pl.BlockSpec(shape, lambda *_: (0,) * len(shape))


def swaps(first, second, axes, count):
    met = []
    for value, start in ((first, 0), (second, 1)):
        edges = [(i, i + 1) for i in range(start, count - 1, 2)]
        met.append(lax.ppermute(value, axes, edges + [(j, i) for i, j in edges]))
    return met


def exchange(parts, axes):
    return lax.all_to_all(parts, axes, 0, 0)


def shown(part, axes, count):
    return exchange(jnp.broadcast_to(part[None], (count,) + part.shape), axes)


def sums_over_all(part):
    inner = shown(part, ("zh", "zl", "core"), 16)
    spread = pl.pallas_call(
        spread_sum_kernel,
        in_specs=[vmem()],
        out_specs=vmem(),
        out_shape=jax.ShapeDtypeStruct(inner.shape, F32),
        compiler_params=params(4),
    )(inner)
    return exchange(spread, PLANE)


def vmem():
    return pl.BlockSpec(memory_space=pltpu.VMEM)


def hbm():
    return pl.BlockSpec(memory_space=pl.ANY)


def swapped(value):
    return lax.ppermute(value, "core", [(0, 1), (1, 0)])


def forward_local(near, feat_t, weight):
    offsets, slots = near.shape
    width = feat_t.shape[0]
    mid, rest = offsets // 3, offsets - offsets // 3
    return pl.pallas_call(
        local_kernel,
        in_specs=[vmem(), vmem(), hbm()],
        out_specs=[vmem()] * 4,
        out_shape=[
            jax.ShapeDtypeStruct((2, mid * width // 2, slots), BF16),
            jax.ShapeDtypeStruct((2, rest * width // 2, slots), BF16),
            jax.ShapeDtypeStruct((width, mid * width), BF16),
            jax.ShapeDtypeStruct((width, rest * width), BF16),
        ],
        scratch_shapes=[pltpu.VMEM((offsets, width, width), BF16), pltpu.SemaphoreType.DMA((3,))],
        compiler_params=params(24),
    )(near, feat_t, weight)


def forward_middle(near, column, part, weight_t):
    return pl.pallas_call(
        middle_kernel,
        in_specs=[vmem()] * 4,
        out_specs=[vmem()] * 2,
        out_shape=[
            jax.ShapeDtypeStruct(part.shape, BF16),
            jax.ShapeDtypeStruct((weight_t.shape[0], near.shape[1]), F32),
        ],
        compiler_params=params(16),
    )(near, column, part, weight_t)


def forward_rest(odd, near, first, second, part, weight_t, pre_t):
    width, slots = pre_t.shape
    return pl.pallas_call(
        forward_kernel,
        in_specs=[smem()] + [vmem()] * 6,
        out_specs=[vmem()] * 3,
        out_shape=[
            jax.ShapeDtypeStruct(part.shape, BF16),
            jax.ShapeDtypeStruct((slots, width), F32),
            jax.ShapeDtypeStruct((2, width), F32),
        ],
        scratch_shapes=[pltpu.VMEM((2,) + first.shape, BF16)],
        compiler_params=params(24),
    )(odd, near, first, second, part, weight_t, pre_t)


def weight_grad_sent(core, counts, pre, dscaled, sums, gamma_row, back_sums, mid, rest, offsets):
    slots, width = pre.shape
    return pl.pallas_call(
        weight_grad_kernel,
        in_specs=[smem(), smem()] + [vmem()] * 7,
        out_specs=[vmem()] * 3,
        out_shape=[
            jax.ShapeDtypeStruct((slots, width), BF16),
            jax.ShapeDtypeStruct((offsets, width // 2, width), BF16),
            jax.ShapeDtypeStruct((2, width), F32),
        ],
        compiler_params=params(16),
    )(core, counts, pre, dscaled, sums, gamma_row, back_sums, mid, rest)


def weight_grad_kept(core, mid, rest, dpre, offsets):
    width = dpre.shape[1]
    return pl.pallas_call(
        other_half_kernel,
        in_specs=[smem()] + [vmem()] * 3,
        out_specs=vmem(),
        out_shape=jax.ShapeDtypeStruct((offsets, width // 2, width), BF16),
        compiler_params=params(16),
    )(core, mid, rest, dpre)


def widened(core, part, held):
    offsets, half, width = part.shape
    rest = [] if held is None else [held]
    return pl.pallas_call(
        own_rows_kernel if held is None else other_rows_kernel,
        in_specs=[smem(), vmem()] + [hbm()] * len(rest),
        out_specs=hbm(),
        out_shape=pltpu.HBM((offsets, 2 * half, width), F32),
        scratch_shapes=[pltpu.VMEM(part.shape, F32), pltpu.SemaphoreType.DMA((offsets // 3,))],
        input_output_aliases={2: 0} if rest else {},
        compiler_params=params(16),
    )(core, part, *rest)


def pool_gradient(odd, near, dpre, weight):
    offsets, slots = near.shape
    groups = offsets // 3
    width = dpre.shape[1]
    rims = slots // 4

    def place(g, odd):
        b = lax.rem(g, 3)
        return (jnp.where(odd[0] == 1, b, 2 - b) * 3 + lax.div(g, 3), 0, 0)

    return pl.pallas_call(
        pool_grad_kernel,
        grid_spec=pltpu.PrefetchScalarGridSpec(
            num_scalar_prefetch=1,
            grid=(groups,),
            in_specs=[
                whole(near.shape),
                whole((slots, width)),
                pl.BlockSpec((3, width, width), lambda g, odd: (g, 0, 0)),
            ],
            out_specs=[whole((slots, width)), pl.BlockSpec((1, rims, width), place)],
        ),
        out_shape=[
            jax.ShapeDtypeStruct((slots, width), F32),
            jax.ShapeDtypeStruct((groups, rims, width), BF16),
        ],
        compiler_params=params(20),
    )(odd, near, dpre, weight)


def on_device(features, conv_weight, gamma, beta, cotangent, counts, rim_rows, neighbours):
    slots, width = features.shape
    rims = rim_rows.shape[0]
    offsets = neighbours.shape[0]
    groups = offsets // 3
    half = width // 2
    core = lax.axis_index("core").astype(jnp.int32)[None]
    odd_x = lax.rem(lax.axis_index(GX), 2).astype(jnp.int32)[None]
    odd_y = lax.rem(lax.axis_index(GY), 2).astype(jnp.int32)[None]
    rows = rim_rows.reshape(1, rims)
    rows, core, odd_x, odd_y = lax.optimization_barrier((rows, core, odd_x, odd_y))
    gamma_row = gamma.reshape(1, width)
    beta_row = beta.reshape(1, width)
    weight = pltpu.with_memory_space_constraint(conv_weight, pltpu.HBM)

    rim, feat_t, near = pl.pallas_call(
        rim_kernel,
        in_specs=[hbm()] * 3,
        out_specs=[vmem()] * 3,
        out_shape=[
            jax.ShapeDtypeStruct((rims, width), BF16),
            jax.ShapeDtypeStruct((width, slots), BF16),
            jax.ShapeDtypeStruct((offsets, slots), jnp.int32),
        ],
        scratch_shapes=[
            pltpu.VMEM((1, rims), jnp.int32),
            pltpu.VMEM((slots, width), BF16),
            pltpu.SemaphoreType.DMA((3,)),
        ],
        compiler_params=params(16),
    )(
        pltpu.with_memory_space_constraint(rows, pltpu.HBM),
        pltpu.with_memory_space_constraint(features, pltpu.HBM),
        pltpu.with_memory_space_constraint(neighbours, pltpu.HBM),
    )
    first, second = swaps(rim, rim, GX, 32)
    local_parts = forward_local(near, feat_t, weight)
    first, second, local_parts = lax.optimization_barrier((first, second, local_parts))
    mid_part, rest_part, mid_weight, rest_weight = local_parts
    column = pl.pallas_call(
        column_kernel,
        in_specs=[smem()] + [vmem()] * 3,
        out_specs=vmem(),
        out_shape=jax.ShapeDtypeStruct((3, rims, width), BF16),
        compiler_params=params(8),
    )(odd_x, rim, first, second)
    first, second = swaps(column, column, GY, 8)
    mid, pre_t = forward_middle(near, column, mid_part, mid_weight)
    rest, pre, stats = forward_rest(odd_y, near, first, second, rest_part, rest_weight, pre_t)

    count_row = jnp.full((1, width), counts[0].astype(F32))
    sums = sums_over_all(jnp.concatenate([stats, count_row, jnp.zeros((1, width), F32)], axis=0))
    activated, dscaled, back = pl.pallas_call(
        activation_kernel,
        in_specs=[smem()] + [vmem()] * 5,
        out_shape=[
            jax.ShapeDtypeStruct((slots, width), BF16),
            jax.ShapeDtypeStruct((slots, width), F32),
            jax.ShapeDtypeStruct((2, width), F32),
        ],
        compiler_params=params(16),
    )(counts, pre, sums, gamma_row, beta_row, cotangent)
    back_sums = sums_over_all(back)

    dpre, send, bn_grads = weight_grad_sent(
        core, counts, pre, dscaled, sums, gamma_row, back_sums, mid, rest, offsets
    )
    met = swapped(send)
    keep = weight_grad_kept(core, mid, rest, dpre, offsets)
    mine = pl.pallas_call(
        met_kernel,
        in_specs=[vmem()] * 2,
        out_specs=hbm(),
        out_shape=pltpu.HBM(keep.shape, BF16),
        scratch_shapes=[pltpu.VMEM(keep.shape, BF16), pltpu.SemaphoreType.DMA((3,))],
        compiler_params=params(8),
    )(keep, met)

    plane_rows = offsets * half // 16
    depth_rows = -(-plane_rows // 64) * 8
    mine = exchange(mine.reshape(16, plane_rows, width), PLANE)
    local, partials = pool_gradient(odd_y, near, dpre, weight)
    gamma_grad, beta_grad = bn_grads[1], bn_grads[0]
    first, second = swaps(partials[:3], partials[6:], GY, 8)
    strip, first, second = pl.pallas_call(
        strip_kernel,
        in_specs=[smem()] + [vmem()] * 3,
        out_specs=[vmem()] * 3,
        out_shape=[
            jax.ShapeDtypeStruct((rims, width), F32),
            jax.ShapeDtypeStruct((rims, width), BF16),
            jax.ShapeDtypeStruct((rims, width), BF16),
        ],
        compiler_params=params(8),
    )(odd_x, partials, first, second)
    mine, local, strip, first, second, gamma_grad, beta_grad = lax.optimization_barrier(
        (mine, local, strip, first, second, gamma_grad, beta_grad)
    )
    mine = pl.pallas_call(
        plane_sum_kernel,
        in_specs=[vmem()],
        out_specs=vmem(),
        out_shape=jax.ShapeDtypeStruct((8 * depth_rows, width), BF16),
        compiler_params=params(8),
    )(mine)
    mine = exchange(mine.reshape(8, depth_rows, width), DEPTH)
    mine = jnp.sum(mine.astype(F32), axis=0).astype(BF16)
    mine = shown(mine, DEPTH, 8).reshape(8 * depth_rows, width)
    mine, first, second = lax.optimization_barrier((mine, first, second))
    first, second = swaps(first, second, GX, 32)
    mine = pl.pallas_call(
        repeat_kernel,
        in_specs=[vmem()],
        out_specs=hbm(),
        out_shape=pltpu.HBM((16, plane_rows, width), BF16),
        scratch_shapes=[pltpu.SemaphoreType.DMA((16,))],
        compiler_params=params(8),
    )(mine)
    mine = exchange(mine, PLANE).reshape(offsets, half, width)
    input_grad = pl.pallas_call(
        input_grad_kernel,
        out_shape=jax.ShapeDtypeStruct((slots, width), BF16),
        compiler_params=params(16),
    )(rows, local, strip, first, second)
    mine, input_grad = lax.optimization_barrier((mine, input_grad))
    other = swapped(mine)
    held = widened(core, mine, None)
    other, held = lax.optimization_barrier((other, held))
    weight_grad = widened(core, other, held)
    return (activated, input_grad, weight_grad, gamma_grad, beta_grad)


def solution(mesh):
    finer = Mesh(mesh.devices.reshape(SIZES), AXES)
    return jax.shard_map(
        on_device,
        mesh=finer,
        in_specs=(P(AXES, None), P(), P(), P(), P(AXES, None), P(AXES), P(AXES), P(None, AXES)),
        out_specs=(P(AXES, None), P(AXES, None), P(), P(), P()),
        check_vma=False,
    )
```

```python
import functools

import jax
import jax.numpy as jnp
from jax import lax
from jax.experimental import pallas as pl
from jax.experimental.pallas import tpu as pltpu
from jax.sharding import Mesh, PartitionSpec as P

AXES = ("x", "zh", "y", "zl", "core")
SIZES = (4, 2, 4, 4, 2)
GX = ("x", "zh", "y")
GY = ("zl", "core")
PLANE = ("x", "y")
DEPTH = ("zl", "zh")
F32 = jnp.float32
BF16 = jnp.bfloat16


def params(mib):
    return pltpu.CompilerParams(vmem_limit_bytes=mib << 20)


def rows_of(first, second, dims):
    return lax.dot_general(first, second, (dims, ((), ())), preferred_element_type=F32)


def rim_kernel(rows_hbm, feat_hbm, near_hbm, rim_ref, feat_t_ref, near_ref, rows_ref, feat_ref, sem):
    copies = [
        pltpu.make_async_copy(rows_hbm, rows_ref, sem.at[0]),
        pltpu.make_async_copy(feat_hbm, feat_ref, sem.at[1]),
        pltpu.make_async_copy(near_hbm, near_ref, sem.at[2]),
    ]
    for copy in copies:
        copy.start()
    slots = feat_ref.shape[0]
    rims = rim_ref.shape[0]
    copies[0].wait()
    slot = lax.broadcasted_iota(jnp.int32, (slots, rims), 0)
    hit = jnp.where(slot == rows_ref[...], 1.0, 0.0).astype(BF16)
    copies[1].wait()
    feat = feat_ref[...]
    rim_ref[...] = rows_of(hit, feat, ((0,), (0,))).astype(BF16)
    feat_t_ref[...] = jnp.transpose(feat)
    copies[2].wait()


def order_of(groups):
    return sorted(range(groups), key=lambda g: g % 3 != 1)


def local_kernel(near_ref, feat_t, weight_hbm, mid_ref, rest_ref, mid_weight_ref, rest_weight_ref, held, sem):
    groups = near_ref.shape[0] // 3
    width, slots = feat_t.shape
    half = width // 2
    copies = [
        pltpu.make_async_copy(
            weight_hbm.at[pl.ds(9 * i, 9)], held.at[pl.ds(9 * i, 9)], sem.at[i]
        )
        for i in range(groups // 3)
    ]
    for copy in copies:
        copy.start()
    slot = lax.broadcasted_iota(jnp.int32, (slots, slots), 0)
    for place, g in enumerate(order_of(groups)):
        part_ref, first = (mid_ref, 0) if place < 3 else (rest_ref, 9)
        hits = [
            jnp.where(slot == near_ref[3 * g + j : 3 * g + j + 1, :], 1.0, 0.0).astype(BF16) for j in range(3)
        ]
        rows = jnp.dot(feat_t[...], jnp.concatenate(hits, axis=1), preferred_element_type=F32).astype(BF16)
        for j in range(3):
            at = (3 * place + j - first) * half
            part_ref[0, at : at + half, :] = rows[:half, j * slots : (j + 1) * slots]
            part_ref[1, at : at + half, :] = rows[half:, j * slots : (j + 1) * slots]
    for copy in copies:
        copy.wait()
    for place, g in enumerate(order_of(groups)):
        out_ref, first = (mid_weight_ref, 0) if place < 3 else (rest_weight_ref, 9)
        count = out_ref.shape[1] // width
        for j in range(3):
            for h in range(2):
                at = (h * count + 3 * place + j - first) * half
                out_ref[:, at : at + half] = jnp.transpose(held[3 * g + j, h * half : (h + 1) * half, :])


def add_rim(near_ref, g, rim, part_ref, rows_ref, first):
    rims, width = rim.shape
    slots = near_ref.shape[1]
    half = width // 2
    slot = lax.broadcasted_iota(jnp.int32, (rims, slots), 0) + (slots + g * rims)
    hits = [
        jnp.where(slot == near_ref[3 * g + j : 3 * g + j + 1, :], 1.0, 0.0).astype(BF16) for j in range(3)
    ]
    rows = jnp.dot(jnp.transpose(rim), jnp.concatenate(hits, axis=1), preferred_element_type=F32).astype(BF16)
    for j in range(3):
        at = (first + j) * half
        for h in range(2):
            found = rows[h * half : (h + 1) * half, j * slots : (j + 1) * slots]
            rows_ref[h, at : at + half, :] = part_ref[h, at : at + half, :] + found


def products_t(weight_t_ref, rows_ref):
    span = weight_t_ref.shape[1] // 2
    return sum(
        jnp.dot(weight_t_ref[:, h * span : (h + 1) * span], rows_ref[h], preferred_element_type=F32)
        for h in range(2)
    )


def middle_kernel(near_ref, column_ref, part_ref, weight_t_ref, rows_ref, pre_t_ref):
    groups = near_ref.shape[0] // 3
    span = part_ref.shape[1] // 3
    for place, g in enumerate(order_of(groups)[:3]):
        if g == groups // 2:
            at = slice(place * span, (place + 1) * span)
            rows_ref[:, at, :] = part_ref[:, at, :]
        else:
            add_rim(near_ref, g, column_ref[g // 3], part_ref, rows_ref, 3 * place)
    pre_t_ref[...] = products_t(weight_t_ref, rows_ref)


def column_kernel(odd_ref, rim_ref, first_ref, second_ref, column_ref):
    column_ref[1] = rim_ref[...]

    @pl.when(odd_ref[0] == 1)
    def _():
        column_ref[0] = first_ref[...]
        column_ref[2] = second_ref[...]

    @pl.when(odd_ref[0] == 0)
    def _():
        column_ref[0] = second_ref[...]
        column_ref[2] = first_ref[...]


def forward_kernel(
    odd_ref, near_ref, first_ref, second_ref, part_ref, weight_t_ref, pre_t_ref, rows_ref, pre_ref, stats_ref, sides
):
    groups = near_ref.shape[0] // 3

    @pl.when(odd_ref[0] == 1)
    def _():
        sides[0] = first_ref[...]
        sides[1] = second_ref[...]

    @pl.when(odd_ref[0] == 0)
    def _():
        sides[0] = second_ref[...]
        sides[1] = first_ref[...]

    for place, g in enumerate(order_of(groups)[3:]):
        add_rim(near_ref, g, sides[g % 3 // 2, g // 3], part_ref, rows_ref, 3 * place)
    pre = jnp.transpose(pre_t_ref[...] + products_t(weight_t_ref, rows_ref))
    pre_ref[...] = pre
    stats_ref[0:1, :] = jnp.sum(pre, axis=0, keepdims=True)
    stats_ref[1:2, :] = jnp.sum(pre * pre, axis=0, keepdims=True)


def moments(sums_ref):
    sums = jnp.sum(sums_ref[...], axis=0)
    total = sums[2:3, :]
    average = sums[0:1, :] / total
    variance = sums[1:2, :] / total - average * average
    return average, 1.0 / jnp.sqrt(variance + 1e-05), total


def activation_kernel(
    count_ref, pre_ref, sums_ref, gamma_ref, beta_ref, cotangent_ref, active_ref, dscaled_ref, stats_ref
):
    slots = pre_ref.shape[0]
    average, inv_std, _ = moments(sums_ref)
    centered = (pre_ref[...] - average) * inv_std
    scaled = gamma_ref[...] * centered + beta_ref[...]
    sig = jax.nn.sigmoid(scaled)
    mask = lax.broadcasted_iota(jnp.int32, pre_ref.shape, 0) < count_ref[0]
    active_ref[...] = jnp.where(mask, scaled * sig, 0.0).astype(BF16)
    dscaled = jnp.where(mask, cotangent_ref[...].astype(F32) * sig * (1.0 + scaled * (1.0 - sig)), 0.0)
    dscaled_ref[...] = dscaled
    stats_ref[0:1, :] = jnp.sum(dscaled, axis=0, keepdims=True)
    stats_ref[1:2, :] = jnp.sum(dscaled * centered, axis=0, keepdims=True)


def half_products(mid_ref, rest_ref, which, dpre, out_ref):
    span = mid_ref.shape[1]
    half = out_ref.shape[1]
    for i in range(3):
        held = mid_ref[which] if i == 0 else rest_ref[which, (i - 1) * span : i * span, :]
        term = jnp.dot(held, dpre, preferred_element_type=F32)
        out_ref[i * (span // half) : (i + 1) * (span // half)] = term.astype(BF16).reshape(
            span // half, half, out_ref.shape[2]
        )


def weight_grad_kernel(
    half_ref, count_ref, pre_ref, dscaled_ref, sums_ref, gamma_ref, back_ref, mid_ref, rest_ref, dpre_ref, send_ref, bn_ref
):
    average, inv_std, total = moments(sums_ref)
    back = jnp.sum(back_ref[...], axis=0)
    bn_ref[...] = back
    centered = (pre_ref[...] - average) * inv_std
    grad = gamma_ref[...] * inv_std * (dscaled_ref[...] - (back[0:1, :] + centered * back[1:2, :]) / total)
    mask = lax.broadcasted_iota(jnp.int32, pre_ref.shape, 0) < count_ref[0]
    dpre = jnp.where(mask, grad, 0.0).astype(BF16)
    dpre_ref[...] = dpre
    half_products(mid_ref, rest_ref, 1 - half_ref[0], dpre, send_ref)


def other_half_kernel(half_ref, mid_ref, rest_ref, dpre_ref, keep_ref):
    half_products(mid_ref, rest_ref, half_ref[0], dpre_ref[...], keep_ref)


def pool_grad_kernel(odd_ref, near_ref, dpre_ref, weight_ref, local_ref, halo_ref):
    step = pl.program_id(0)
    slots, width = dpre_ref.shape
    rims = halo_ref.shape[1]
    pool_rows = slots + rims
    slot = lax.broadcasted_iota(jnp.int32, (pool_rows, slots), 0)
    hits, contribs = [], []
    for j in range(3):
        row = near_ref[pl.ds(3 * step + j, 1), :]
        row = jnp.where(row >= slots, row - step * rims, row)
        hits.append(jnp.where(slot == row, 1.0, 0.0).astype(BF16))
        contribs.append(rows_of(dpre_ref[...], weight_ref[j], ((1,), (1,))).astype(BF16))
    total = jnp.dot(
        jnp.concatenate(hits, axis=1), jnp.concatenate(contribs, axis=0), preferred_element_type=F32
    )
    halo_ref[0] = total[slots:, :].astype(BF16)

    @pl.when(step == 0)
    def _():
        local_ref[...] = total[:slots, :]

    @pl.when(step > 0)
    def _():
        local_ref[...] += total[:slots, :]


def strip_kernel(odd_ref, parts_ref, first_ref, second_ref, strip_ref, out_first_ref, out_second_ref):
    strips = [
        parts_ref[3 + a].astype(F32) + first_ref[a].astype(F32) + second_ref[a].astype(F32)
        for a in range(3)
    ]
    strip_ref[...] = strips[1]
    odd = odd_ref[0] == 1
    out_first_ref[...] = jnp.where(odd, strips[0], strips[2]).astype(BF16)
    out_second_ref[...] = jnp.where(odd, strips[2], strips[0]).astype(BF16)


def input_grad_kernel(rows_ref, local_ref, strip_ref, first_ref, second_ref, out_ref):
    slots = local_ref.shape[0]
    rims = strip_ref.shape[0]
    slot = lax.broadcasted_iota(jnp.int32, (slots, rims), 0)
    hit = jnp.where(slot == rows_ref[...], 1.0, 0.0).astype(BF16)
    final = strip_ref[...] + first_ref[...].astype(F32) + second_ref[...].astype(F32)
    high = final.astype(BF16)
    low = (final - high.astype(F32)).astype(BF16)
    added = jnp.dot(hit, high, preferred_element_type=F32) + jnp.dot(hit, low, preferred_element_type=F32)
    out_ref[...] = (local_ref[...] + added).astype(BF16)


def spread_sum_kernel(parts_ref, out_ref):
    out_ref[...] = jnp.broadcast_to(jnp.sum(parts_ref[...], axis=0, keepdims=True), out_ref.shape)


def plane_sum_kernel(parts_ref, out_ref):
    rows = parts_ref.shape[1]
    out_ref[rows:, :] = jnp.zeros((out_ref.shape[0] - rows, out_ref.shape[1]), BF16)
    out_ref[:rows, :] = jnp.sum(parts_ref[...].astype(F32), axis=0).astype(BF16)


def met_kernel(keep_ref, met_ref, out_hbm, total, sem):
    span = total.shape[0] // 3
    copies = []
    for n in range(3):
        at = pl.ds(n * span, span)
        total[at] = (keep_ref[at].astype(F32) + met_ref[at].astype(F32)).astype(BF16)
        copies.append(pltpu.make_async_copy(total.at[at], out_hbm.at[at], sem.at[n]))
        copies[-1].start()
    for copy in copies:
        copy.wait()


def repeat_kernel(part_ref, out_hbm, sem):
    count, rows, _ = out_hbm.shape
    copies = [
        pltpu.make_async_copy(part_ref.at[pl.ds(0, rows)], out_hbm.at[n], sem.at[n]) for n in range(count)
    ]
    for copy in copies:
        copy.start()
    for copy in copies:
        copy.wait()


def put_rows(part_ref, place, out_hbm, wide, sem):
    half = part_ref.shape[1]
    rows = pl.ds(pl.multiple_of(place * half, half), half)
    copies = []
    for n, g in enumerate(order_of(part_ref.shape[0] // 3)):
        at = pl.ds(3 * n, 3)
        wide[at] = part_ref[at].astype(F32)
        copies.append(pltpu.make_async_copy(wide.at[at], out_hbm.at[pl.ds(3 * g, 3), rows], sem.at[n]))
        copies[-1].start()
    for copy in copies:
        copy.wait()


def own_rows_kernel(half_ref, part_ref, out_hbm, wide, sem):
    put_rows(part_ref, half_ref[0], out_hbm, wide, sem)


def other_rows_kernel(half_ref, part_ref, held_hbm, out_hbm, wide, sem):
    put_rows(part_ref, 1 - half_ref[0], out_hbm, wide, sem)


def smem():
    return pl.BlockSpec(memory_space=pltpu.SMEM)


def whole(shape):
    return pl.BlockSpec(shape, lambda *_: (0,) * len(shape))


def swaps(first, second, axes, count):
    met = []
    for value, start in ((first, 0), (second, 1)):
        edges = [(i, i + 1) for i in range(start, count - 1, 2)]
        met.append(lax.ppermute(value, axes, edges + [(j, i) for i, j in edges]))
    return met


def exchange(parts, axes):
    return lax.all_to_all(parts, axes, 0, 0)


def shown(part, axes, count):
    return exchange(jnp.broadcast_to(part[None], (count,) + part.shape), axes)


def sums_over_all(part):
    inner = shown(part, ("zh", "zl", "core"), 16)
    spread = pl.pallas_call(
        spread_sum_kernel,
        in_specs=[vmem()],
        out_specs=vmem(),
        out_shape=jax.ShapeDtypeStruct(inner.shape, F32),
        compiler_params=params(4),
    )(inner)
    return exchange(spread, PLANE)


def vmem():
    return pl.BlockSpec(memory_space=pltpu.VMEM)


def hbm():
    return pl.BlockSpec(memory_space=pl.ANY)


def swapped(value):
    return lax.ppermute(value, "core", [(0, 1), (1, 0)])


def forward_local(near, feat_t, weight):
    offsets, slots = near.shape
    width = feat_t.shape[0]
    mid, rest = offsets // 3, offsets - offsets // 3
    return pl.pallas_call(
        local_kernel,
        in_specs=[vmem(), vmem(), hbm()],
        out_specs=[vmem()] * 4,
        out_shape=[
            jax.ShapeDtypeStruct((2, mid * width // 2, slots), BF16),
            jax.ShapeDtypeStruct((2, rest * width // 2, slots), BF16),
            jax.ShapeDtypeStruct((width, mid * width), BF16),
            jax.ShapeDtypeStruct((width, rest * width), BF16),
        ],
        scratch_shapes=[pltpu.VMEM((offsets, width, width), BF16), pltpu.SemaphoreType.DMA((3,))],
        compiler_params=params(24),
    )(near, feat_t, weight)


def forward_middle(near, column, part, weight_t):
    return pl.pallas_call(
        middle_kernel,
        in_specs=[vmem()] * 4,
        out_specs=[vmem()] * 2,
        out_shape=[
            jax.ShapeDtypeStruct(part.shape, BF16),
            jax.ShapeDtypeStruct((weight_t.shape[0], near.shape[1]), F32),
        ],
        compiler_params=params(16),
    )(near, column, part, weight_t)


def forward_rest(odd, near, first, second, part, weight_t, pre_t):
    width, slots = pre_t.shape
    return pl.pallas_call(
        forward_kernel,
        in_specs=[smem()] + [vmem()] * 6,
        out_specs=[vmem()] * 3,
        out_shape=[
            jax.ShapeDtypeStruct(part.shape, BF16),
            jax.ShapeDtypeStruct((slots, width), F32),
            jax.ShapeDtypeStruct((2, width), F32),
        ],
        scratch_shapes=[pltpu.VMEM((2,) + first.shape, BF16)],
        compiler_params=params(24),
    )(odd, near, first, second, part, weight_t, pre_t)


def weight_grad_sent(core, counts, pre, dscaled, sums, gamma_row, back_sums, mid, rest, offsets):
    slots, width = pre.shape
    return pl.pallas_call(
        weight_grad_kernel,
        in_specs=[smem(), smem()] + [vmem()] * 7,
        out_specs=[vmem()] * 3,
        out_shape=[
            jax.ShapeDtypeStruct((slots, width), BF16),
            jax.ShapeDtypeStruct((offsets, width // 2, width), BF16),
            jax.ShapeDtypeStruct((2, width), F32),
        ],
        compiler_params=params(16),
    )(core, counts, pre, dscaled, sums, gamma_row, back_sums, mid, rest)


def weight_grad_kept(core, mid, rest, dpre, offsets):
    width = dpre.shape[1]
    return pl.pallas_call(
        other_half_kernel,
        in_specs=[smem()] + [vmem()] * 3,
        out_specs=vmem(),
        out_shape=jax.ShapeDtypeStruct((offsets, width // 2, width), BF16),
        compiler_params=params(16),
    )(core, mid, rest, dpre)


def widened(core, part, held):
    offsets, half, width = part.shape
    rest = [] if held is None else [held]
    return pl.pallas_call(
        own_rows_kernel if held is None else other_rows_kernel,
        in_specs=[smem(), vmem()] + [hbm()] * len(rest),
        out_specs=hbm(),
        out_shape=pltpu.HBM((offsets, 2 * half, width), F32),
        scratch_shapes=[pltpu.VMEM(part.shape, F32), pltpu.SemaphoreType.DMA((offsets // 3,))],
        input_output_aliases={2: 0} if rest else {},
        compiler_params=params(16),
    )(core, part, *rest)


def pool_gradient(odd, near, dpre, weight):
    offsets, slots = near.shape
    groups = offsets // 3
    width = dpre.shape[1]
    rims = slots // 4

    def place(g, odd):
        b = lax.rem(g, 3)
        return (jnp.where(odd[0] == 1, b, 2 - b) * 3 + lax.div(g, 3), 0, 0)

    return pl.pallas_call(
        pool_grad_kernel,
        grid_spec=pltpu.PrefetchScalarGridSpec(
            num_scalar_prefetch=1,
            grid=(groups,),
            in_specs=[
                whole(near.shape),
                whole((slots, width)),
                pl.BlockSpec((3, width, width), lambda g, odd: (g, 0, 0)),
            ],
            out_specs=[whole((slots, width)), pl.BlockSpec((1, rims, width), place)],
        ),
        out_shape=[
            jax.ShapeDtypeStruct((slots, width), F32),
            jax.ShapeDtypeStruct((groups, rims, width), BF16),
        ],
        compiler_params=params(20),
    )(odd, near, dpre, weight)


def on_device(features, conv_weight, gamma, beta, cotangent, counts, rim_rows, neighbours):
    slots, width = features.shape
    rims = rim_rows.shape[0]
    offsets = neighbours.shape[0]
    groups = offsets // 3
    half = width // 2
    core = lax.axis_index("core").astype(jnp.int32)[None]
    odd_x = lax.rem(lax.axis_index(GX), 2).astype(jnp.int32)[None]
    odd_y = lax.rem(lax.axis_index(GY), 2).astype(jnp.int32)[None]
    rows = rim_rows.reshape(1, rims)
    rows, core, odd_x, odd_y = lax.optimization_barrier((rows, core, odd_x, odd_y))
    gamma_row = gamma.reshape(1, width)
    beta_row = beta.reshape(1, width)
    weight = pltpu.with_memory_space_constraint(conv_weight, pltpu.HBM)

    rim, feat_t, near = pl.pallas_call(
        rim_kernel,
        in_specs=[hbm()] * 3,
        out_specs=[vmem()] * 3,
        out_shape=[
            jax.ShapeDtypeStruct((rims, width), BF16),
            jax.ShapeDtypeStruct((width, slots), BF16),
            jax.ShapeDtypeStruct((offsets, slots), jnp.int32),
        ],
        scratch_shapes=[
            pltpu.VMEM((1, rims), jnp.int32),
            pltpu.VMEM((slots, width), BF16),
            pltpu.SemaphoreType.DMA((3,)),
        ],
        compiler_params=params(16),
    )(
        pltpu.with_memory_space_constraint(rows, pltpu.HBM),
        pltpu.with_memory_space_constraint(features, pltpu.HBM),
        pltpu.with_memory_space_constraint(neighbours, pltpu.HBM),
    )
    first, second = swaps(rim, rim, GX, 32)
    local_parts = forward_local(near, feat_t, weight)
    first, second, local_parts = lax.optimization_barrier((first, second, local_parts))
    mid_part, rest_part, mid_weight, rest_weight = local_parts
    column = pl.pallas_call(
        column_kernel,
        in_specs=[smem()] + [vmem()] * 3,
        out_specs=vmem(),
        out_shape=jax.ShapeDtypeStruct((3, rims, width), BF16),
        compiler_params=params(8),
    )(odd_x, rim, first, second)
    first, second = swaps(column, column, GY, 8)
    mid, pre_t = forward_middle(near, column, mid_part, mid_weight)
    rest, pre, stats = forward_rest(odd_y, near, first, second, rest_part, rest_weight, pre_t)

    count_row = jnp.full((1, width), counts[0].astype(F32))
    sums = sums_over_all(jnp.concatenate([stats, count_row, jnp.zeros((1, width), F32)], axis=0))
    activated, dscaled, back = pl.pallas_call(
        activation_kernel,
        in_specs=[smem()] + [vmem()] * 5,
        out_shape=[
            jax.ShapeDtypeStruct((slots, width), BF16),
            jax.ShapeDtypeStruct((slots, width), F32),
            jax.ShapeDtypeStruct((2, width), F32),
        ],
        compiler_params=params(16),
    )(counts, pre, sums, gamma_row, beta_row, cotangent)
    back_sums = sums_over_all(back)

    dpre, send, bn_grads = weight_grad_sent(
        core, counts, pre, dscaled, sums, gamma_row, back_sums, mid, rest, offsets
    )
    met = swapped(send)
    keep = weight_grad_kept(core, mid, rest, dpre, offsets)
    mine = pl.pallas_call(
        met_kernel,
        in_specs=[vmem()] * 2,
        out_specs=hbm(),
        out_shape=pltpu.HBM(keep.shape, BF16),
        scratch_shapes=[pltpu.VMEM(keep.shape, BF16), pltpu.SemaphoreType.DMA((3,))],
        compiler_params=params(8),
    )(keep, met)

    plane_rows = offsets * half // 16
    depth_rows = -(-plane_rows // 64) * 8
    mine = exchange(mine.reshape(16, plane_rows, width), PLANE)
    local, partials = pool_gradient(odd_y, near, dpre, weight)
    gamma_grad, beta_grad = bn_grads[1], bn_grads[0]
    first, second = swaps(partials[:3], partials[6:], GY, 8)
    strip, first, second = pl.pallas_call(
        strip_kernel,
        in_specs=[smem()] + [vmem()] * 3,
        out_specs=[vmem()] * 3,
        out_shape=[
            jax.ShapeDtypeStruct((rims, width), F32),
            jax.ShapeDtypeStruct((rims, width), BF16),
            jax.ShapeDtypeStruct((rims, width), BF16),
        ],
        compiler_params=params(8),
    )(odd_x, partials, first, second)
    mine, local, strip, first, second, gamma_grad, beta_grad = lax.optimization_barrier(
        (mine, local, strip, first, second, gamma_grad, beta_grad)
    )
    mine = pl.pallas_call(
        plane_sum_kernel,
        in_specs=[vmem()],
        out_specs=vmem(),
        out_shape=jax.ShapeDtypeStruct((8 * depth_rows, width), BF16),
        compiler_params=params(8),
    )(mine)
    mine = exchange(mine.reshape(8, depth_rows, width), DEPTH)
    mine = jnp.sum(mine.astype(F32), axis=0).astype(BF16)
    mine = shown(mine, DEPTH, 8).reshape(8 * depth_rows, width)
    mine, first, second = lax.optimization_barrier((mine, first, second))
    first, second = swaps(first, second, GX, 32)
    mine = pl.pallas_call(
        repeat_kernel,
        in_specs=[vmem()],
        out_specs=hbm(),
        out_shape=pltpu.HBM((16, plane_rows, width), BF16),
        scratch_shapes=[pltpu.SemaphoreType.DMA((16,))],
        compiler_params=params(8),
    )(mine)
    mine = exchange(mine, PLANE).reshape(offsets, half, width)
    mine, first, second = lax.optimization_barrier((mine, first, second))
    other = swapped(mine)
    input_grad = pl.pallas_call(
        input_grad_kernel,
        out_shape=jax.ShapeDtypeStruct((slots, width), BF16),
        compiler_params=params(16),
    )(rows, local, strip, first, second)
    held = widened(core, mine, None)
    other, held, input_grad = lax.optimization_barrier((other, held, input_grad))
    weight_grad = widened(core, other, held)
    return (activated, input_grad, weight_grad, gamma_grad, beta_grad)


def solution(mesh):
    finer = Mesh(mesh.devices.reshape(SIZES), AXES)
    return jax.shard_map(
        on_device,
        mesh=finer,
        in_specs=(P(AXES, None), P(), P(), P(), P(AXES, None), P(AXES), P(AXES), P(None, AXES)),
        out_specs=(P(AXES, None), P(AXES, None), P(), P(), P()),
        check_vma=False,
    )
```

```python
import functools

import jax
import jax.numpy as jnp
from jax import lax
from jax.experimental import pallas as pl
from jax.experimental.pallas import tpu as pltpu
from jax.sharding import Mesh, PartitionSpec as P

AXES = ("x", "zh", "y", "zl", "core")
SIZES = (4, 2, 4, 4, 2)
GX = ("x", "zh", "y")
GY = ("zl", "core")
PLANE = ("x", "y")
DEPTH = ("zl", "zh")
F32 = jnp.float32
BF16 = jnp.bfloat16


def params(mib):
    return pltpu.CompilerParams(vmem_limit_bytes=mib << 20)


def rows_of(first, second, dims):
    return lax.dot_general(first, second, (dims, ((), ())), preferred_element_type=F32)


def rim_kernel(rows_hbm, feat_hbm, near_hbm, rim_ref, feat_t_ref, near_ref, rows_ref, feat_ref, sem):
    copies = [
        pltpu.make_async_copy(rows_hbm, rows_ref, sem.at[0]),
        pltpu.make_async_copy(feat_hbm, feat_ref, sem.at[1]),
        pltpu.make_async_copy(near_hbm, near_ref, sem.at[2]),
    ]
    for copy in copies:
        copy.start()
    slots = feat_ref.shape[0]
    rims = rim_ref.shape[0]
    copies[0].wait()
    slot = lax.broadcasted_iota(jnp.int32, (slots, rims), 0)
    hit = jnp.where(slot == rows_ref[...], 1.0, 0.0).astype(BF16)
    copies[1].wait()
    feat = feat_ref[...]
    rim_ref[...] = rows_of(hit, feat, ((0,), (0,))).astype(BF16)
    feat_t_ref[...] = jnp.transpose(feat)
    copies[2].wait()


def order_of(groups):
    return sorted(range(groups), key=lambda g: g % 3 != 1)


def weight_copies(weight_hbm, held, sem, chosen):
    copies = [
        pltpu.make_async_copy(weight_hbm.at[pl.ds(3 * g, 3)], held.at[pl.ds(3 * n, 3)], sem.at[n])
        for n, g in enumerate(chosen)
    ]
    for copy in copies:
        copy.start()
    return copies


def turn_weights(copies, held, out_ref):
    count, width, _ = held.shape
    half = width // 2
    for n, copy in enumerate(copies):
        copy.wait()
        for k in range(3 * n, 3 * n + 3):
            for h in range(2):
                at = (h * count + k) * half
                out_ref[:, at : at + half] = jnp.transpose(held[k, h * half : (h + 1) * half, :])


def local_kernel(near_ref, feat_t, weight_hbm, mid_ref, rest_ref, mid_weight_ref, held, sem):
    groups = near_ref.shape[0] // 3
    width, slots = feat_t.shape
    half = width // 2
    order = order_of(groups)
    copies = weight_copies(weight_hbm, held, sem, order[:3])
    slot = lax.broadcasted_iota(jnp.int32, (slots, slots), 0)
    for place, g in enumerate(order):
        part_ref, first = (mid_ref, 0) if place < 3 else (rest_ref, 9)
        hits = [
            jnp.where(slot == near_ref[3 * g + j : 3 * g + j + 1, :], 1.0, 0.0).astype(BF16) for j in range(3)
        ]
        rows = jnp.dot(feat_t[...], jnp.concatenate(hits, axis=1), preferred_element_type=F32).astype(BF16)
        for j in range(3):
            at = (3 * place + j - first) * half
            part_ref[0, at : at + half, :] = rows[:half, j * slots : (j + 1) * slots]
            part_ref[1, at : at + half, :] = rows[half:, j * slots : (j + 1) * slots]
    turn_weights(copies, held, mid_weight_ref)


def add_rim(near_ref, g, rim, part_ref, rows_ref, first):
    rims, width = rim.shape
    slots = near_ref.shape[1]
    half = width // 2
    slot = lax.broadcasted_iota(jnp.int32, (rims, slots), 0) + (slots + g * rims)
    hits = [
        jnp.where(slot == near_ref[3 * g + j : 3 * g + j + 1, :], 1.0, 0.0).astype(BF16) for j in range(3)
    ]
    rows = jnp.dot(jnp.transpose(rim), jnp.concatenate(hits, axis=1), preferred_element_type=F32).astype(BF16)
    for j in range(3):
        at = (first + j) * half
        for h in range(2):
            found = rows[h * half : (h + 1) * half, j * slots : (j + 1) * slots]
            rows_ref[h, at : at + half, :] = part_ref[h, at : at + half, :] + found


def products_t(weight_t_ref, rows_ref):
    span = weight_t_ref.shape[1] // 2
    return sum(
        jnp.dot(weight_t_ref[:, h * span : (h + 1) * span], rows_ref[h], preferred_element_type=F32)
        for h in range(2)
    )


def middle_kernel(
    near_ref, column_ref, part_ref, weight_t_ref, weight_hbm, rows_ref, pre_t_ref, rest_weight_ref, held, sem
):
    groups = near_ref.shape[0] // 3
    copies = weight_copies(weight_hbm, held, sem, order_of(groups)[3:])
    span = part_ref.shape[1] // 3
    for place, g in enumerate(order_of(groups)[:3]):
        if g == groups // 2:
            at = slice(place * span, (place + 1) * span)
            rows_ref[:, at, :] = part_ref[:, at, :]
        else:
            add_rim(near_ref, g, column_ref[g // 3], part_ref, rows_ref, 3 * place)
    pre_t_ref[...] = products_t(weight_t_ref, rows_ref)
    turn_weights(copies, held, rest_weight_ref)


def column_kernel(odd_ref, rim_ref, first_ref, second_ref, column_ref):
    column_ref[1] = rim_ref[...]

    @pl.when(odd_ref[0] == 1)
    def _():
        column_ref[0] = first_ref[...]
        column_ref[2] = second_ref[...]

    @pl.when(odd_ref[0] == 0)
    def _():
        column_ref[0] = second_ref[...]
        column_ref[2] = first_ref[...]


def forward_kernel(
    odd_ref, near_ref, first_ref, second_ref, part_ref, weight_t_ref, pre_t_ref, rows_ref, pre_ref, stats_ref, sides
):
    groups = near_ref.shape[0] // 3

    @pl.when(odd_ref[0] == 1)
    def _():
        sides[0] = first_ref[...]
        sides[1] = second_ref[...]

    @pl.when(odd_ref[0] == 0)
    def _():
        sides[0] = second_ref[...]
        sides[1] = first_ref[...]

    for place, g in enumerate(order_of(groups)[3:]):
        add_rim(near_ref, g, sides[g % 3 // 2, g // 3], part_ref, rows_ref, 3 * place)
    pre = jnp.transpose(pre_t_ref[...] + products_t(weight_t_ref, rows_ref))
    pre_ref[...] = pre
    stats_ref[0:1, :] = jnp.sum(pre, axis=0, keepdims=True)
    stats_ref[1:2, :] = jnp.sum(pre * pre, axis=0, keepdims=True)


def moments(sums_ref):
    sums = jnp.sum(sums_ref[...], axis=0)
    total = sums[2:3, :]
    average = sums[0:1, :] / total
    variance = sums[1:2, :] / total - average * average
    return average, 1.0 / jnp.sqrt(variance + 1e-05), total


def activation_kernel(
    count_ref, pre_ref, sums_ref, gamma_ref, beta_ref, cotangent_ref, active_ref, dscaled_ref, stats_ref
):
    slots = pre_ref.shape[0]
    average, inv_std, _ = moments(sums_ref)
    centered = (pre_ref[...] - average) * inv_std
    scaled = gamma_ref[...] * centered + beta_ref[...]
    sig = jax.nn.sigmoid(scaled)
    mask = lax.broadcasted_iota(jnp.int32, pre_ref.shape, 0) < count_ref[0]
    active_ref[...] = jnp.where(mask, scaled * sig, 0.0).astype(BF16)
    dscaled = jnp.where(mask, cotangent_ref[...].astype(F32) * sig * (1.0 + scaled * (1.0 - sig)), 0.0)
    dscaled_ref[...] = dscaled
    stats_ref[0:1, :] = jnp.sum(dscaled, axis=0, keepdims=True)
    stats_ref[1:2, :] = jnp.sum(dscaled * centered, axis=0, keepdims=True)


def half_products(mid_ref, rest_ref, which, dpre, out_ref):
    span = mid_ref.shape[1]
    half = out_ref.shape[1]
    for i in range(3):
        held = mid_ref[which] if i == 0 else rest_ref[which, (i - 1) * span : i * span, :]
        term = jnp.dot(held, dpre, preferred_element_type=F32)
        out_ref[i * (span // half) : (i + 1) * (span // half)] = term.astype(BF16).reshape(
            span // half, half, out_ref.shape[2]
        )


def weight_grad_kernel(
    half_ref, count_ref, pre_ref, dscaled_ref, sums_ref, gamma_ref, back_ref, mid_ref, rest_ref, dpre_ref, send_ref, bn_ref
):
    average, inv_std, total = moments(sums_ref)
    back = jnp.sum(back_ref[...], axis=0)
    bn_ref[...] = back
    centered = (pre_ref[...] - average) * inv_std
    grad = gamma_ref[...] * inv_std * (dscaled_ref[...] - (back[0:1, :] + centered * back[1:2, :]) / total)
    mask = lax.broadcasted_iota(jnp.int32, pre_ref.shape, 0) < count_ref[0]
    dpre = jnp.where(mask, grad, 0.0).astype(BF16)
    dpre_ref[...] = dpre
    half_products(mid_ref, rest_ref, 1 - half_ref[0], dpre, send_ref)


def other_half_kernel(half_ref, mid_ref, rest_ref, dpre_ref, keep_ref):
    half_products(mid_ref, rest_ref, half_ref[0], dpre_ref[...], keep_ref)


def pool_grad_kernel(odd_ref, near_ref, dpre_ref, weight_ref, local_ref, halo_ref):
    step = pl.program_id(0)
    slots, width = dpre_ref.shape
    rims = halo_ref.shape[1]
    pool_rows = slots + rims
    slot = lax.broadcasted_iota(jnp.int32, (pool_rows, slots), 0)
    hits, contribs = [], []
    for j in range(3):
        row = near_ref[pl.ds(3 * step + j, 1), :]
        row = jnp.where(row >= slots, row - step * rims, row)
        hits.append(jnp.where(slot == row, 1.0, 0.0).astype(BF16))
        contribs.append(rows_of(dpre_ref[...], weight_ref[j], ((1,), (1,))).astype(BF16))
    total = jnp.dot(
        jnp.concatenate(hits, axis=1), jnp.concatenate(contribs, axis=0), preferred_element_type=F32
    )
    halo_ref[0] = total[slots:, :].astype(BF16)

    @pl.when(step == 0)
    def _():
        local_ref[...] = total[:slots, :]

    @pl.when(step > 0)
    def _():
        local_ref[...] += total[:slots, :]


def strip_kernel(odd_ref, parts_ref, first_ref, second_ref, strip_ref, out_first_ref, out_second_ref):
    strips = [
        parts_ref[3 + a].astype(F32) + first_ref[a].astype(F32) + second_ref[a].astype(F32)
        for a in range(3)
    ]
    strip_ref[...] = strips[1]
    odd = odd_ref[0] == 1
    out_first_ref[...] = jnp.where(odd, strips[0], strips[2]).astype(BF16)
    out_second_ref[...] = jnp.where(odd, strips[2], strips[0]).astype(BF16)


def input_grad_kernel(rows_ref, local_ref, strip_ref, first_ref, second_ref, out_ref):
    slots = local_ref.shape[0]
    rims = strip_ref.shape[0]
    slot = lax.broadcasted_iota(jnp.int32, (slots, rims), 0)
    hit = jnp.where(slot == rows_ref[...], 1.0, 0.0).astype(BF16)
    final = strip_ref[...] + first_ref[...].astype(F32) + second_ref[...].astype(F32)
    high = final.astype(BF16)
    low = (final - high.astype(F32)).astype(BF16)
    added = jnp.dot(hit, high, preferred_element_type=F32) + jnp.dot(hit, low, preferred_element_type=F32)
    out_ref[...] = (local_ref[...] + added).astype(BF16)


def spread_sum_kernel(parts_ref, out_ref):
    out_ref[...] = jnp.broadcast_to(jnp.sum(parts_ref[...], axis=0, keepdims=True), out_ref.shape)


def plane_sum_kernel(parts_ref, out_ref):
    rows = parts_ref.shape[1]
    out_ref[rows:, :] = jnp.zeros((out_ref.shape[0] - rows, out_ref.shape[1]), BF16)
    out_ref[:rows, :] = jnp.sum(parts_ref[...].astype(F32), axis=0).astype(BF16)


def met_kernel(keep_ref, met_ref, out_hbm, total, sem):
    span = total.shape[0] // 3
    copies = []
    for n in range(3):
        at = pl.ds(n * span, span)
        total[at] = (keep_ref[at].astype(F32) + met_ref[at].astype(F32)).astype(BF16)
        copies.append(pltpu.make_async_copy(total.at[at], out_hbm.at[at], sem.at[n]))
        copies[-1].start()
    for copy in copies:
        copy.wait()


def repeat_kernel(part_ref, out_hbm, sem):
    count, rows, _ = out_hbm.shape
    copies = [
        pltpu.make_async_copy(part_ref.at[pl.ds(0, rows)], out_hbm.at[n], sem.at[n]) for n in range(count)
    ]
    for copy in copies:
        copy.start()
    for copy in copies:
        copy.wait()


def put_rows(part_ref, place, out_hbm, wide, sem):
    half = part_ref.shape[1]
    rows = pl.ds(pl.multiple_of(place * half, half), half)
    copies = []
    for n, g in enumerate(order_of(part_ref.shape[0] // 3)):
        at = pl.ds(3 * n, 3)
        wide[at] = part_ref[at].astype(F32)
        copies.append(pltpu.make_async_copy(wide.at[at], out_hbm.at[pl.ds(3 * g, 3), rows], sem.at[n]))
        copies[-1].start()
    for copy in copies:
        copy.wait()


def own_rows_kernel(half_ref, part_ref, out_hbm, wide, sem):
    put_rows(part_ref, half_ref[0], out_hbm, wide, sem)


def other_rows_kernel(half_ref, part_ref, held_hbm, out_hbm, wide, sem):
    put_rows(part_ref, 1 - half_ref[0], out_hbm, wide, sem)


def smem():
    return pl.BlockSpec(memory_space=pltpu.SMEM)


def whole(shape):
    return pl.BlockSpec(shape, lambda *_: (0,) * len(shape))


def swaps(first, second, axes, count):
    met = []
    for value, start in ((first, 0), (second, 1)):
        edges = [(i, i + 1) for i in range(start, count - 1, 2)]
        met.append(lax.ppermute(value, axes, edges + [(j, i) for i, j in edges]))
    return met


def exchange(parts, axes):
    return lax.all_to_all(parts, axes, 0, 0)


def shown(part, axes, count):
    return exchange(jnp.broadcast_to(part[None], (count,) + part.shape), axes)


def sums_over_all(part):
    inner = shown(part, ("zh", "zl", "core"), 16)
    spread = pl.pallas_call(
        spread_sum_kernel,
        in_specs=[vmem()],
        out_specs=vmem(),
        out_shape=jax.ShapeDtypeStruct(inner.shape, F32),
        compiler_params=params(4),
    )(inner)
    return exchange(spread, PLANE)


def vmem():
    return pl.BlockSpec(memory_space=pltpu.VMEM)


def hbm():
    return pl.BlockSpec(memory_space=pl.ANY)


def swapped(value):
    return lax.ppermute(value, "core", [(0, 1), (1, 0)])


def forward_local(near, feat_t, weight):
    offsets, slots = near.shape
    width = feat_t.shape[0]
    mid, rest = offsets // 3, offsets - offsets // 3
    return pl.pallas_call(
        local_kernel,
        in_specs=[vmem(), vmem(), hbm()],
        out_specs=[vmem()] * 3,
        out_shape=[
            jax.ShapeDtypeStruct((2, mid * width // 2, slots), BF16),
            jax.ShapeDtypeStruct((2, rest * width // 2, slots), BF16),
            jax.ShapeDtypeStruct((width, mid * width), BF16),
        ],
        scratch_shapes=[pltpu.VMEM((mid, width, width), BF16), pltpu.SemaphoreType.DMA((mid // 3,))],
        compiler_params=params(24),
    )(near, feat_t, weight)


def forward_middle(near, column, part, weight_t, weight):
    offsets, slots = near.shape
    width = weight_t.shape[0]
    rest = offsets - offsets // 3
    return pl.pallas_call(
        middle_kernel,
        in_specs=[vmem()] * 4 + [hbm()],
        out_specs=[vmem()] * 3,
        out_shape=[
            jax.ShapeDtypeStruct(part.shape, BF16),
            jax.ShapeDtypeStruct((width, slots), F32),
            jax.ShapeDtypeStruct((width, rest * width), BF16),
        ],
        scratch_shapes=[pltpu.VMEM((rest, width, width), BF16), pltpu.SemaphoreType.DMA((rest // 3,))],
        compiler_params=params(16),
    )(near, column, part, weight_t, weight)


def forward_rest(odd, near, first, second, part, weight_t, pre_t):
    width, slots = pre_t.shape
    return pl.pallas_call(
        forward_kernel,
        in_specs=[smem()] + [vmem()] * 6,
        out_specs=[vmem()] * 3,
        out_shape=[
            jax.ShapeDtypeStruct(part.shape, BF16),
            jax.ShapeDtypeStruct((slots, width), F32),
            jax.ShapeDtypeStruct((2, width), F32),
        ],
        scratch_shapes=[pltpu.VMEM((2,) + first.shape, BF16)],
        compiler_params=params(24),
    )(odd, near, first, second, part, weight_t, pre_t)


def weight_grad_sent(core, counts, pre, dscaled, sums, gamma_row, back_sums, mid, rest, offsets):
    slots, width = pre.shape
    return pl.pallas_call(
        weight_grad_kernel,
        in_specs=[smem(), smem()] + [vmem()] * 7,
        out_specs=[vmem()] * 3,
        out_shape=[
            jax.ShapeDtypeStruct((slots, width), BF16),
            jax.ShapeDtypeStruct((offsets, width // 2, width), BF16),
            jax.ShapeDtypeStruct((2, width), F32),
        ],
        compiler_params=params(16),
    )(core, counts, pre, dscaled, sums, gamma_row, back_sums, mid, rest)


def weight_grad_kept(core, mid, rest, dpre, offsets):
    width = dpre.shape[1]
    return pl.pallas_call(
        other_half_kernel,
        in_specs=[smem()] + [vmem()] * 3,
        out_specs=vmem(),
        out_shape=jax.ShapeDtypeStruct((offsets, width // 2, width), BF16),
        compiler_params=params(16),
    )(core, mid, rest, dpre)


def widened(core, part, held):
    offsets, half, width = part.shape
    rest = [] if held is None else [held]
    return pl.pallas_call(
        own_rows_kernel if held is None else other_rows_kernel,
        in_specs=[smem(), vmem()] + [hbm()] * len(rest),
        out_specs=hbm(),
        out_shape=pltpu.HBM((offsets, 2 * half, width), F32),
        scratch_shapes=[pltpu.VMEM(part.shape, F32), pltpu.SemaphoreType.DMA((offsets // 3,))],
        input_output_aliases={2: 0} if rest else {},
        compiler_params=params(16),
    )(core, part, *rest)


def pool_gradient(odd, near, dpre, weight):
    offsets, slots = near.shape
    groups = offsets // 3
    width = dpre.shape[1]
    rims = slots // 4

    def place(g, odd):
        b = lax.rem(g, 3)
        return (jnp.where(odd[0] == 1, b, 2 - b) * 3 + lax.div(g, 3), 0, 0)

    return pl.pallas_call(
        pool_grad_kernel,
        grid_spec=pltpu.PrefetchScalarGridSpec(
            num_scalar_prefetch=1,
            grid=(groups,),
            in_specs=[
                whole(near.shape),
                whole((slots, width)),
                pl.BlockSpec((3, width, width), lambda g, odd: (g, 0, 0)),
            ],
            out_specs=[whole((slots, width)), pl.BlockSpec((1, rims, width), place)],
        ),
        out_shape=[
            jax.ShapeDtypeStruct((slots, width), F32),
            jax.ShapeDtypeStruct((groups, rims, width), BF16),
        ],
        compiler_params=params(20),
    )(odd, near, dpre, weight)


def on_device(features, conv_weight, gamma, beta, cotangent, counts, rim_rows, neighbours):
    slots, width = features.shape
    rims = rim_rows.shape[0]
    offsets = neighbours.shape[0]
    groups = offsets // 3
    half = width // 2
    core = lax.axis_index("core").astype(jnp.int32)[None]
    odd_x = lax.rem(lax.axis_index(GX), 2).astype(jnp.int32)[None]
    odd_y = lax.rem(lax.axis_index(GY), 2).astype(jnp.int32)[None]
    rows = rim_rows.reshape(1, rims)
    rows, core, odd_x, odd_y = lax.optimization_barrier((rows, core, odd_x, odd_y))
    gamma_row = gamma.reshape(1, width)
    beta_row = beta.reshape(1, width)
    weight = pltpu.with_memory_space_constraint(conv_weight, pltpu.HBM)

    rim, feat_t, near = pl.pallas_call(
        rim_kernel,
        in_specs=[hbm()] * 3,
        out_specs=[vmem()] * 3,
        out_shape=[
            jax.ShapeDtypeStruct((rims, width), BF16),
            jax.ShapeDtypeStruct((width, slots), BF16),
            jax.ShapeDtypeStruct((offsets, slots), jnp.int32),
        ],
        scratch_shapes=[
            pltpu.VMEM((1, rims), jnp.int32),
            pltpu.VMEM((slots, width), BF16),
            pltpu.SemaphoreType.DMA((3,)),
        ],
        compiler_params=params(16),
    )(
        pltpu.with_memory_space_constraint(rows, pltpu.HBM),
        pltpu.with_memory_space_constraint(features, pltpu.HBM),
        pltpu.with_memory_space_constraint(neighbours, pltpu.HBM),
    )
    first, second = swaps(rim, rim, GX, 32)
    local_parts = forward_local(near, feat_t, weight)
    first, second, local_parts = lax.optimization_barrier((first, second, local_parts))
    mid_part, rest_part, mid_weight = local_parts
    column = pl.pallas_call(
        column_kernel,
        in_specs=[smem()] + [vmem()] * 3,
        out_specs=vmem(),
        out_shape=jax.ShapeDtypeStruct((3, rims, width), BF16),
        compiler_params=params(8),
    )(odd_x, rim, first, second)
    first, second = swaps(column, column, GY, 8)
    mid, pre_t, rest_weight = forward_middle(near, column, mid_part, mid_weight, weight)
    rest, pre, stats = forward_rest(odd_y, near, first, second, rest_part, rest_weight, pre_t)

    count_row = jnp.full((1, width), counts[0].astype(F32))
    sums = sums_over_all(jnp.concatenate([stats, count_row, jnp.zeros((1, width), F32)], axis=0))
    activated, dscaled, back = pl.pallas_call(
        activation_kernel,
        in_specs=[smem()] + [vmem()] * 5,
        out_shape=[
            jax.ShapeDtypeStruct((slots, width), BF16),
            jax.ShapeDtypeStruct((slots, width), F32),
            jax.ShapeDtypeStruct((2, width), F32),
        ],
        compiler_params=params(16),
    )(counts, pre, sums, gamma_row, beta_row, cotangent)
    back_sums = sums_over_all(back)

    dpre, send, bn_grads = weight_grad_sent(
        core, counts, pre, dscaled, sums, gamma_row, back_sums, mid, rest, offsets
    )
    met = swapped(send)
    keep = weight_grad_kept(core, mid, rest, dpre, offsets)
    mine = pl.pallas_call(
        met_kernel,
        in_specs=[vmem()] * 2,
        out_specs=hbm(),
        out_shape=pltpu.HBM(keep.shape, BF16),
        scratch_shapes=[pltpu.VMEM(keep.shape, BF16), pltpu.SemaphoreType.DMA((3,))],
        compiler_params=params(8),
    )(keep, met)

    plane_rows = offsets * half // 16
    depth_rows = -(-plane_rows // 64) * 8
    mine = exchange(mine.reshape(16, plane_rows, width), PLANE)
    local, partials = pool_gradient(odd_y, near, dpre, weight)
    gamma_grad, beta_grad = bn_grads[1], bn_grads[0]
    first, second = swaps(partials[:3], partials[6:], GY, 8)
    strip, first, second = pl.pallas_call(
        strip_kernel,
        in_specs=[smem()] + [vmem()] * 3,
        out_specs=[vmem()] * 3,
        out_shape=[
            jax.ShapeDtypeStruct((rims, width), F32),
            jax.ShapeDtypeStruct((rims, width), BF16),
            jax.ShapeDtypeStruct((rims, width), BF16),
        ],
        compiler_params=params(8),
    )(odd_x, partials, first, second)
    mine, local, strip, first, second, gamma_grad, beta_grad = lax.optimization_barrier(
        (mine, local, strip, first, second, gamma_grad, beta_grad)
    )
    mine = pl.pallas_call(
        plane_sum_kernel,
        in_specs=[vmem()],
        out_specs=vmem(),
        out_shape=jax.ShapeDtypeStruct((8 * depth_rows, width), BF16),
        compiler_params=params(8),
    )(mine)
    mine = exchange(mine.reshape(8, depth_rows, width), DEPTH)
    mine = jnp.sum(mine.astype(F32), axis=0).astype(BF16)
    mine = shown(mine, DEPTH, 8).reshape(8 * depth_rows, width)
    mine, first, second = lax.optimization_barrier((mine, first, second))
    first, second = swaps(first, second, GX, 32)
    mine = pl.pallas_call(
        repeat_kernel,
        in_specs=[vmem()],
        out_specs=hbm(),
        out_shape=pltpu.HBM((16, plane_rows, width), BF16),
        scratch_shapes=[pltpu.SemaphoreType.DMA((16,))],
        compiler_params=params(8),
    )(mine)
    mine = exchange(mine, PLANE).reshape(offsets, half, width)
    mine, first, second = lax.optimization_barrier((mine, first, second))
    other = swapped(mine)
    input_grad = pl.pallas_call(
        input_grad_kernel,
        out_shape=jax.ShapeDtypeStruct((slots, width), BF16),
        compiler_params=params(16),
    )(rows, local, strip, first, second)
    held = widened(core, mine, None)
    other, held, input_grad = lax.optimization_barrier((other, held, input_grad))
    weight_grad = widened(core, other, held)
    return (activated, input_grad, weight_grad, gamma_grad, beta_grad)


def solution(mesh):
    finer = Mesh(mesh.devices.reshape(SIZES), AXES)
    return jax.shard_map(
        on_device,
        mesh=finer,
        in_specs=(P(AXES, None), P(), P(), P(), P(AXES, None), P(AXES), P(AXES), P(None, AXES)),
        out_specs=(P(AXES, None), P(AXES, None), P(), P(), P()),
        check_vma=False,
    )
```
